128 devices in a mesh: ctx: 32 (over z, x, y_lo), tp: 4 (over y_hi, core).
Axes of the slice: x: 4, y: 4 (y_hi: 2, y_lo: 2; y = y_hi * 2 + y_lo), z: 4, core: 2. Of those that a mesh axis runs over, the one named last changes fastest.
Arguments:
- queries: bfloat16 [16384, 2048], P('ctx', 'tp'), may hold values from -40 to 40
- keys: bfloat16 [16384, 2048], P('ctx', 'tp'), may hold values from -40 to 40
- values: bfloat16 [16384, 2048], P('ctx', 'tp'), may hold values from -6 to 6
- out_weight: bfloat16 [2048, 4096], P('tp'), may hold values from -0.1875 to 0.1875
- doc_lengths: int32 [64], replicated, may hold values from 1 to 2048, 16384 in all
- layout: int32 [64], replicated, may hold values from 0 to 63, each once
Outputs:
- mixed: bfloat16 [16384, 4096], P('ctx', 'tp')
- log_totals: float32 [16, 16384], P('tp', 'ctx')
The draws below stay inside these ranges and needn't reach their ends.
Inputs may be any that keep to these rules, and one draw needn't show every extreme that they name: `layout`: every block number appears once. `doc_lengths`: the lengths sum to 16384; the longest is exactly 2048.
All inputs are finite; a program needn't handle non-finite values.
Results may differ from the reference program's by a relative error of at most 0.012.
Values may be sent and summed in bfloat16 or wider, within the bound.
A program may use at most 192 MiB of HBM per device.

```python
import math
import jax
import jax.numpy as jnp
import numpy as np
from jax import lax

D = 4096
HEAD_DIM = 128
HEADS = 16
HALF = 256
SEQ = 16384
BLOCKS = 64
DOCS = 64
LONGEST = 2048


def paired_rows(key):
    shape = (SEQ, HEADS * HEAD_DIM)
    key_part = jax.random.normal(jax.random.fold_in(key, 11), shape, jnp.float32)
    query_part = jax.random.normal(jax.random.fold_in(key, 12), shape, jnp.float32)
    return (jnp.clip(query_part, -40.0, 40.0), jnp.clip(key_part, -40.0, 40.0))


def draw_queries(key, part):
    return paired_rows(key)[0].astype(jnp.bfloat16)


def draw_keys(key, part):
    return paired_rows(key)[1].astype(jnp.bfloat16)


def spiked(entries, stream_key, source, target, parts, factor):
    owner, partner = [(jnp.arange(entries.shape[dim]) // (entries.shape[dim] // parts)).reshape([-1 if axis == dim else 1 for axis in range(entries.ndim)]) for dim in (source, target)]
    chosen = jax.random.permutation(stream_key, parts)[partner]
    strong = (owner == chosen) | (owner == (partner + parts // 2) % parts)
    return jnp.where(strong, factor * entries, entries)


def steps_of(rng, extent, cuts, smallest, high):
    factor_of = 1.0
    for dim, parts in cuts:
        heights = jax.random.uniform(jax.random.fold_in(jax.random.fold_in(rng, 6), dim), (parts,), jnp.float32, smallest / len(cuts), high / len(cuts))
        factor_of = factor_of * jnp.repeat(jnp.exp(heights), extent[dim] // parts).reshape((-1,) + (1,) * (len(extent) - 1 - dim))
    return factor_of


def length_profile(amount, total, bound, skew):
    loads = [(1 << 20) // math.isqrt(standing ** skew) + 1 for standing in range(2, amount + 1)]
    surplus, counts = total - bound - (amount - 1), [1] * (amount - 1)
    while surplus > 0:
        movable = [i for i in range(amount - 1) if counts[i] < bound]
        mass, remaining = sum([loads[i] for i in movable]), surplus
        for i in movable:
            more = min(bound - counts[i], max(1, remaining * loads[i] // mass), surplus)
            counts[i] = counts[i] + more
            surplus = surplus - more
    return np.array([bound] + counts)


def ragged_sizes(key, count, total, most, lean):
    if count == 2:
        one = jax.random.randint(key, (), max(1, total - most), min(most, total - 1) + 1)
        return jnp.stack([one, total - one])
    sizes = jnp.asarray(length_profile(count, total, most, lean), jnp.int32)
    couples = (count - 1) // 2
    giver, sink = sizes[1:1 + 2 * couples:2], sizes[2:2 + 2 * couples:2]
    room = jnp.minimum(giver - 1, most - sink)
    moved = jax.random.randint(jax.random.fold_in(key, 1), (couples,), 0, 1 << 20) % (room + 1)
    sizes = sizes.at[1:1 + 2 * couples:2].set(giver - moved).at[2:2 + 2 * couples:2].set(sink + moved)
    return sizes[jax.random.permutation(jax.random.fold_in(key, 2), count)]


def noise(rng, shape, width, limit, cuts=(), kind=jnp.bfloat16):
    values = jax.random.normal(rng, shape, jnp.float32) * width
    if len(cuts) > 0:
        values = steps_of(rng, shape, cuts, -0.22, 0.18) * values
    return jnp.clip(values, min=-limit, max=limit).astype(kind)


def noise_with(own_key, shape, width, limit, pieces, heavy, held_as=jnp.bfloat16):
    array = width * jax.random.normal(own_key, shape, jnp.float32)
    if pieces:
        array = array * steps_of(own_key, shape, pieces, -0.22, 0.18)
    return jnp.clip(spiked(array, jax.random.fold_in(own_key, 3), *heavy), -limit, limit).astype(held_as)


def setup_inputs(seed: int = 0) -> dict:
    key_list = jax.random.split(jax.random.key(seed), 7)
    return {
        "queries": draw_queries(jax.random.fold_in(key_list[6], 71), 0),
        "keys": draw_keys(jax.random.fold_in(key_list[6], 71), 0),
        "values": noise(key_list[2], (SEQ, HEADS * HEAD_DIM), 1.0, 6.0, ((0, 32), (1, 4))),
        "out_weight": noise_with(key_list[3], (HEADS * HEAD_DIM, D), (HEADS * HEAD_DIM) ** -0.5, 0.1875, ((0, 4),), (0, 1, 4, 2.0)),
        "doc_lengths": ragged_sizes(key_list[4], DOCS, SEQ, LONGEST, 2).astype(jnp.int32),
        "layout": jax.random.permutation(key_list[5], BLOCKS).astype(jnp.int32),
    }


def reference(queries, keys, values, out_weight, doc_lengths, layout):
    seq = queries.shape[0]
    rows = jnp.arange(seq, dtype=jnp.int32)
    position = (layout[rows // HALF] * HALF + rows % HALF).astype(jnp.int32)
    starts = (jnp.cumsum(doc_lengths) - doc_lengths).astype(jnp.int32)
    document = (jnp.sum((starts[None, :] <= position[:, None]).astype(jnp.int32), axis=1) - 1).astype(jnp.int32)
    key_all = keys.astype(jnp.float32).reshape(seq, HEADS, HEAD_DIM)
    value_all = values.astype(jnp.float32).reshape(seq, HEADS, HEAD_DIM)
    blk = min(512, seq)
    scale = 1.0 / (HEAD_DIM ** 0.5)

    def one_block(index):
        first = (index * blk).astype(jnp.int32)
        query_blk = lax.dynamic_slice_in_dim(queries, first, blk, 0).astype(jnp.float32).reshape(blk, HEADS, HEAD_DIM)
        query_pos = lax.dynamic_slice_in_dim(position, first, blk, 0)
        query_doc = lax.dynamic_slice_in_dim(document, first, blk, 0)
        scores = jnp.einsum('qhd,khd->hqk', query_blk, key_all) * scale
        allowed = (document[None, :] == query_doc[:, None]) & (position[None, :] <= query_pos[:, None])
        scores = jnp.where(allowed[None], scores, -1e30)
        top = jnp.max(scores, axis=-1)
        weights = jnp.where(allowed[None], jnp.exp(scores - top[..., None]), 0.0)
        totals = jnp.sum(weights, axis=-1)
        summed = jnp.einsum('hqk,khd->qhd', weights.astype(jnp.bfloat16).astype(jnp.float32), value_all)
        attended = (summed / totals.T[:, :, None]).reshape(blk, HEADS * HEAD_DIM).astype(jnp.bfloat16)
        return attended, top + jnp.log(totals)

    attended, logs = lax.map(one_block, jnp.arange(seq // blk, dtype=jnp.int32))
    attended = attended.reshape(seq, HEADS * HEAD_DIM)
    log_totals = jnp.transpose(logs, (1, 0, 2)).reshape(HEADS, seq)
    mixed = jnp.dot(attended, out_weight, preferred_element_type=jnp.float32).astype(jnp.bfloat16)
    return mixed, log_totals
```

```python
import math

import jax
import jax.numpy as jnp
from jax import lax
from jax.experimental import pallas as pl
from jax.experimental.pallas import tpu as pltpu
from jax.sharding import PartitionSpec as P

HEAD = 128
MESH = pl.DeviceIdType.MESH
ORDER = (0, 1, 3, 2)
LOG2E = math.log2(math.e)


def ctx_of(core, s, r, y):
    return s * (8 - 6 * core) + r * (2 + 6 * core) + y


def my_place():
    ctx, tp = lax.axis_index("ctx"), lax.axis_index("tp")
    z, x, y = lax.div(ctx, 8), lax.rem(lax.div(ctx, 2), 4), lax.rem(ctx, 2)
    core, high = lax.rem(tp, 2), lax.div(tp, 2)
    s = z * (1 - core) + x * core
    r = x * (1 - core) + z * core
    return tp, core, high, s, r, y


def head_columns(s):
    return pl.ds(pl.multiple_of(s * HEAD, HEAD), HEAD)


def gather_kernel(q, k, v, qh, kv, own_sem, s_send, s_recv, g_send, g_recv):
    tp, core, high, s, r, y = my_place()
    left, right, other = lax.rem(r + 3, 4), lax.rem(r + 1, 4), 1 - y
    g_me = r * 2 + y

    def device(s_, r_, y_):
        return (ctx_of(core, s_, r_, y_), tp)

    def spread_from(i):
        return lax.rem(s + 4 - i, 4)

    barrier = pltpu.get_barrier_semaphore()
    partners = [device(lax.rem(s + i, 4), r, y) for i in (1, 2, 3)]
    partners += [device(s, left, y), device(s, right, y), device(s, r, other)]
    for partner in partners:
        pl.semaphore_signal(barrier, inc=1, device_id=partner, device_id_type=MESH)

    own = [
        pltpu.make_async_copy(k.at[:, head_columns(s)], kv.at[g_me, s, 0], own_sem.at[0]),
        pltpu.make_async_copy(v.at[:, head_columns(s)], kv.at[g_me, s, 1], own_sem.at[1]),
        pltpu.make_async_copy(q.at[:, head_columns(s)], qh.at[s], own_sem.at[2]),
    ]
    for copy in own:
        copy.start()
    pl.semaphore_wait(barrier, 6)

    def spread(i, a):
        to = lax.rem(s + i, 4)
        src = (k, v, q)[a].at[:, head_columns(to)]
        dst = qh.at[s] if a == 2 else kv.at[g_me, s, a]
        return pltpu.make_async_remote_copy(
            src_ref=src,
            dst_ref=dst,
            send_sem=s_send.at[i - 1, a],
            recv_sem=s_recv.at[i - 1, a],
            device_id=device(to, r, y),
            device_id_type=MESH,
        )

    sends = []
    for a in (0, 1):
        for i in (1, 3, 2):
            copy = spread(i, a)
            copy.start()
            sends.append(copy)

    def ring(t, j, rel, origin_r, origin_y, to_r, to_y):
        slot = kv.at[origin_r * 2 + origin_y, spread_from(ORDER[t]), j]
        return pltpu.make_async_remote_copy(
            src_ref=slot,
            dst_ref=slot,
            send_sem=g_send.at[t, j, rel],
            recv_sem=g_recv.at[t, j, rel],
            device_id=device(s, to_r, to_y),
            device_id_type=MESH,
        )

    def send(*args):
        copy = ring(*args)
        copy.start()
        sends.append(copy)

    def arrived(t, j, rel):
        ring(t, j, rel, r, y, right, y).wait_recv()

    for t in range(len(ORDER) + 2):
        if t < 4:
            for j in (0, 1):
                if ORDER[t] == 0:
                    own[j].wait()
                else:
                    spread(ORDER[t], j).wait_recv()
                send(t, j, 0, r, y, r, other)
                send(t, j, 1, r, y, right, y)
                send(t, j, 2, r, y, left, y)
        if t == 3:
            for i in (1, 3, 2):
                copy = spread(i, 2)
                copy.start()
                sends.append(copy)
        if 0 <= t - 1 < 4:
            for j in (0, 1):
                arrived(t - 1, j, 0)
                send(t - 1, j, 3, r, other, right, y)
                send(t - 1, j, 4, r, other, left, y)
            for j in (0, 1):
                arrived(t - 1, j, 1 + j)
                if j == 0:
                    send(t - 1, j, 5, left, y, right, y)
                else:
                    send(t - 1, j, 5, right, y, left, y)
        if 0 <= t - 2 < 4:
            for j in (0, 1):
                arrived(t - 2, j, 3 + j)
                if j == 0:
                    send(t - 2, j, 6, left, other, right, y)
                else:
                    send(t - 2, j, 6, right, other, left, y)
    for t in range(4):
        for j in (0, 1):
            for rel in (2 - j, 4 - j, 5, 6):
                arrived(t, j, rel)
    own[2].wait()
    for i in (1, 3, 2):
        spread(i, 2).wait_recv()
    for copy in sends:
        copy.wait_send()


def gather(q, k, v):
    rows = q.shape[0]
    anywhere = pl.BlockSpec(memory_space=pl.ANY)
    return pl.pallas_call(
        gather_kernel,
        name="spread_and_gather",
        out_shape=(
            jax.ShapeDtypeStruct((4, rows, HEAD), q.dtype),
            jax.ShapeDtypeStruct((8, 4, 2, rows, HEAD), q.dtype),
        ),
        in_specs=[anywhere] * 3,
        out_specs=(anywhere, anywhere),
        scratch_shapes=[
            pltpu.SemaphoreType.DMA((3,)),
            pltpu.SemaphoreType.DMA((3, 3)),
            pltpu.SemaphoreType.DMA((3, 3)),
            pltpu.SemaphoreType.DMA((4, 2, 7)),
            pltpu.SemaphoreType.DMA((4, 2, 7)),
        ],
        compiler_params=pltpu.CompilerParams(collective_id=0, has_side_effects=True),
    )(q, k, v)


def attend_kernel(lengths, layout, q, kv, out, logs, start, where_is, doc_at, top, total, summed):
    _, core, _, _, r, y = my_place()
    blocks, docs = layout.shape[0], lengths.shape[0]
    half = q.shape[1] // 2
    scale = 1.0 / math.sqrt(HEAD)

    def place(p, _):
        where_is[layout[p]] = p
        return 0

    lax.fori_loop(0, blocks, place, 0)

    def walk(j, at):
        start[j] = at
        end = at + lengths[j]

        def mark(b, _):
            doc_at[b] = j
            return 0

        lax.fori_loop(lax.div(at + half - 1, half), lax.div(end + half - 1, half), mark, 0)
        return end

    start[docs] = lax.fori_loop(0, docs, walk, 0)

    def one(u, _):
        s_q, h_q = lax.div(u, 2), lax.rem(u, 2)
        block = layout[ctx_of(core, s_q, r, y) * 2 + h_q]
        base = block * half
        first_doc = doc_at[block]
        rows = pl.ds(pl.multiple_of(h_q * half, half), half)
        query = q[s_q, rows, :]
        q_pos = base + lax.broadcasted_iota(jnp.int32, (1, half), 1)

        def doc_start(state):
            j, low = state
            at = start[j]
            return j + 1, jnp.where(q_pos >= at, at, low)

        _, low = lax.while_loop(
            lambda state: start[state[0]] < base + half,
            doc_start,
            (first_doc + 1, jnp.full((1, half), start[first_doc], jnp.int32)),
        )
        first_block = lax.div(start[first_doc], half)
        top[...] = jnp.full(top.shape, -1e30, jnp.float32)
        total[...] = jnp.zeros(total.shape, jnp.float32)
        summed[...] = jnp.zeros(summed.shape, jnp.float32)

        def step(n, _):
            key_block = block - n
            p = where_is[key_block]
            d, h_k = lax.div(p, 2), lax.rem(p, 2)
            z, x, y_k = lax.div(d, 8), lax.rem(lax.div(d, 2), 4), lax.rem(d, 2)
            s_k = z * (1 - core) + x * core
            r_k = x * (1 - core) + z * core
            key_rows = pl.ds(pl.multiple_of(h_k * half, half), half)
            key = kv[r_k * 2 + y_k, s_k, 0, key_rows, :]
            value = kv[r_k * 2 + y_k, s_k, 1, key_rows, :]
            scores = lax.dot_general(
                key, query, (((1,), (1,)), ((), ())), preferred_element_type=jnp.float32
            )
            k_pos = key_block * half + lax.broadcasted_iota(jnp.int32, (half, half), 0)
            scores = jnp.where((k_pos >= low) & (k_pos <= q_pos), scores, -1e30)
            old = top[...]
            new = jnp.maximum(old, jnp.max(scores, axis=0, keepdims=True))
            weights = jnp.exp2((scores - new) * (scale * LOG2E))
            factor = jnp.exp2((old - new) * (scale * LOG2E))
            top[...] = new
            total[...] = total[...] * factor + jnp.sum(weights, axis=0, keepdims=True)
            summed[...] = summed[...] * factor + lax.dot_general(
                value,
                weights.astype(jnp.bfloat16),
                (((0,), (0,)), ((), ())),
                preferred_element_type=jnp.float32,
            )
            return 0

        lax.fori_loop(0, block - first_block + 1, step, 0)
        out[s_q, rows, :] = (summed[...] / total[...]).T.astype(out.dtype)
        logs[s_q, :, rows] = top[...] * scale + jnp.log(total[...])
        return 0

    lax.fori_loop(0, 8, one, 0)


def attend(lengths, layout, q, kv):
    rows = q.shape[1]
    small, near = pl.BlockSpec(memory_space=pltpu.SMEM), pl.BlockSpec(memory_space=pltpu.VMEM)
    return pl.pallas_call(
        attend_kernel,
        name="attend",
        out_shape=(
            jax.ShapeDtypeStruct((4, rows, HEAD), q.dtype),
            jax.ShapeDtypeStruct((4, 1, rows), jnp.float32),
        ),
        in_specs=[small, small, near, near],
        out_specs=(near, near),
        scratch_shapes=[
            pltpu.SMEM((lengths.shape[0] + 1,), jnp.int32),
            pltpu.SMEM((layout.shape[0],), jnp.int32),
            pltpu.SMEM((layout.shape[0],), jnp.int32),
            pltpu.VMEM((1, rows // 2), jnp.float32),
            pltpu.VMEM((1, rows // 2), jnp.float32),
            pltpu.VMEM((HEAD, rows // 2), jnp.float32),
        ],
        compiler_params=pltpu.CompilerParams(vmem_limit_bytes=40 * 1024 * 1024),
    )(lengths, layout, q, kv)


CHUNKS = 4


def project_kernel(
    o, logs, w, mixed, log_out,
    w_near, att, logs_in, own_sum, c_out, c_in, y_out, y_in,
    w_sem, own_sem, a_send, a_recv, l_send, l_recv, c_send, c_recv, y_send, y_recv,
):
    tp, core, high, s, r, y = my_place()
    me = lax.axis_index("ctx")
    rows, columns = mixed.shape
    part = rows // CHUNKS
    targets = ((1 - high) * 2 + 1 - core, (1 - high) * 2 + core, high * 2 + 1 - core, tp)
    loads = []
    for n, target in enumerate(targets):
        at = pl.ds(pl.multiple_of(target * columns, columns), columns)
        copy = pltpu.make_async_copy(w.at[:, at], w_near.at[n], w_sem.at[n])
        copy.start()
        loads.append(copy)
    mate, across = (me, targets[2]), (me, targets[1])
    barrier = pltpu.get_barrier_semaphore()
    partners = [(ctx_of(core, lax.rem(s + i, 4), r, y), tp) for i in (1, 2, 3)] + [mate, across]
    for partner in partners:
        pl.semaphore_signal(barrier, inc=1, device_id=partner, device_id_type=MESH)
    own = [
        pltpu.make_async_copy(o.at[s], att.at[:, head_columns(s)], own_sem.at[0]),
        pltpu.make_async_copy(logs.at[s], logs_in.at[s], own_sem.at[1]),
    ]
    for copy in own:
        copy.start()
    pl.semaphore_wait(barrier, 5)

    sends = []

    def remote(src, dst, send_sem, recv_sem, to):
        return pltpu.make_async_remote_copy(
            src_ref=src, dst_ref=dst, send_sem=send_sem, recv_sem=recv_sem,
            device_id=to, device_id_type=MESH,
        )

    back, back_logs = [], []
    for i in (2, 1, 3):
        to = lax.rem(s + i, 4)
        device = (ctx_of(core, to, r, y), tp)
        back.append(
            remote(o.at[to], att.at[:, head_columns(s)], a_send.at[i - 1], a_recv.at[i - 1], device)
        )
        back_logs.append(
            remote(logs.at[to], logs_in.at[s], l_send.at[i - 1], l_recv.at[i - 1], device)
        )
    for copy in back + back_logs:
        copy.start()
        sends.append(copy)
    own[0].wait()
    for copy in back:
        copy.wait_recv()

    def chunk(c):
        return pl.ds(c * part, part)

    def product(c, n):
        return jnp.dot(att[chunk(c), :], w_near[n], preferred_element_type=jnp.float32)

    def to_mate(c, m):
        return remote(
            c_out.at[m, chunk(c)], c_in.at[m, chunk(c)], c_send.at[m, c], c_recv.at[m, c], mate
        )

    def to_across(c):
        return remote(y_out.at[chunk(c)], y_in.at[chunk(c)], y_send.at[c], y_recv.at[c], across)

    loads[0].wait()
    for c in range(CHUNKS):
        c_out[0, chunk(c), :] = product(c, 0).astype(jnp.bfloat16)
        copy = to_mate(c, 0)
        copy.start()
        sends.append(copy)
    loads[1].wait()
    for c in range(CHUNKS):
        mine = product(c, 1)
        to_mate(c, 0).wait_recv()
        y_out[chunk(c), :] = (mine + c_in[0, chunk(c), :].astype(jnp.float32)).astype(jnp.bfloat16)
        copy = to_across(c)
        copy.start()
        sends.append(copy)
    loads[2].wait()
    for c in range(CHUNKS):
        c_out[1, chunk(c), :] = product(c, 2).astype(jnp.bfloat16)
        copy = to_mate(c, 1)
        copy.start()
        sends.append(copy)
    loads[3].wait()
    for c in range(CHUNKS):
        mine = product(c, 3)
        to_mate(c, 1).wait_recv()
        own_sum[chunk(c), :] = mine + c_in[1, chunk(c), :].astype(jnp.float32)
    own[1].wait()
    for copy in back_logs:
        copy.wait_recv()
    for h in range(4):
        log_out[h : h + 1, :] = logs_in[h]
    for c in range(CHUNKS):
        to_across(c).wait_recv()
        mixed[chunk(c), :] = (own_sum[chunk(c), :] + y_in[chunk(c), :].astype(jnp.float32)).astype(
            jnp.bfloat16
        )
    for copy in sends:
        copy.wait_send()


def project(o, logs, w):
    rows, depth, columns = o.shape[1], w.shape[0], w.shape[1] // 4
    anywhere, near = pl.BlockSpec(memory_space=pl.ANY), pl.BlockSpec(memory_space=pltpu.VMEM)
    dma = pltpu.SemaphoreType.DMA
    return pl.pallas_call(
        project_kernel,
        name="return_and_project",
        out_shape=(
            jax.ShapeDtypeStruct((rows, columns), jnp.bfloat16),
            jax.ShapeDtypeStruct((4, rows), jnp.float32),
        ),
        in_specs=[anywhere, anywhere, anywhere],
        out_specs=(near, near),
        scratch_shapes=[
            pltpu.VMEM((4, depth, columns), jnp.bfloat16),
            pltpu.VMEM((rows, depth), jnp.bfloat16),
            pltpu.VMEM((4, 1, rows), jnp.float32),
            pltpu.VMEM((rows, columns), jnp.float32),
            pltpu.VMEM((2, rows, columns), jnp.bfloat16),
            pltpu.VMEM((2, rows, columns), jnp.bfloat16),
            pltpu.VMEM((rows, columns), jnp.bfloat16),
            pltpu.VMEM((rows, columns), jnp.bfloat16),
            dma((4,)), dma((2,)), dma((3,)), dma((3,)), dma((3,)), dma((3,)),
            dma((2, CHUNKS)), dma((2, CHUNKS)), dma((CHUNKS,)), dma((CHUNKS,)),
        ],
        compiler_params=pltpu.CompilerParams(
            collective_id=1, has_side_effects=True, vmem_limit_bytes=40 * 1024 * 1024
        ),
    )(o, logs, w)


def local(queries, keys, values, out_weight, doc_lengths, layout):
    qh, kv = gather(queries, keys, values)
    o, logs = attend(doc_lengths, layout, qh, kv)
    return project(o, logs, out_weight)


def solution(mesh):
    placed = (P("ctx", "tp"), P("ctx", "tp"), P("ctx", "tp"), P("tp", None), P(), P())
    return jax.shard_map(
        local,
        mesh=mesh,
        in_specs=placed,
        out_specs=(P("ctx", "tp"), P("tp", "ctx")),
        check_vma=False,
    )
```

```python
import math

import jax
import jax.numpy as jnp
from jax import lax
from jax.experimental import pallas as pl
from jax.experimental.pallas import tpu as pltpu
from jax.sharding import PartitionSpec as P

HEAD = 128
MESH = pl.DeviceIdType.MESH
SCALE = 1.0 / math.sqrt(HEAD)
LOG2E = math.log2(math.e)
STREAMS = 4
LEAST = -1e29
VMEM_BYTES = 40 * 1024 * 1024


def ctx_of(core, p, r, y):
    return p * (8 - 6 * core) + r * (2 + 6 * core) + y


def split_ctx(ctx, core):
    z, x, y = lax.div(ctx, 8), lax.rem(lax.div(ctx, 2), 4), lax.rem(ctx, 2)
    return z * (1 - core) + x * core, x * (1 - core) + z * core, y


def pair_bit(p):
    return lax.rem(lax.div(p + 1, 2), 2)


def member_place(pair, m):
    bit = lax.rem(m, 2)
    return bit + pair * (3 - 2 * bit), lax.div(m, 2)


class Place:
    def __init__(self):
        self.ctx, self.tp = lax.axis_index("ctx"), lax.axis_index("tp")
        self.core, self.high = lax.rem(self.tp, 2), lax.div(self.tp, 2)
        self.p, self.r, self.y = split_ctx(self.ctx, self.core)
        self.pair, self.bit = lax.div(self.p, 2), pair_bit(self.p)
        self.m = self.y * 2 + self.bit

    def member(self, i):
        bit = 1 - self.bit if i % 2 else self.bit
        y = 1 - self.y if i // 2 else self.y
        return y * 2 + bit

    def at_member(self, m):
        p, y = member_place(self.pair, m)
        return (ctx_of(self.core, p, self.r, y), self.tp)

    def at_ring(self, r):
        return (ctx_of(self.core, self.p, r, self.y), self.tp)

    def at_twin(self):
        return (ctx_of(self.core, 3 - self.p, self.r, self.y), self.tp)


def head_columns(m):
    return pl.ds(pl.multiple_of(m * HEAD, HEAD), HEAD)


def remote(src, dst, send_sem, recv_sem, to):
    return pltpu.make_async_remote_copy(
        src_ref=src, dst_ref=dst, send_sem=send_sem, recv_sem=recv_sem,
        device_id=to, device_id_type=MESH,
    )


def greet(partners):
    barrier = pltpu.get_barrier_semaphore()
    for partner in partners:
        pl.semaphore_signal(barrier, inc=1, device_id=partner, device_id_type=MESH)
    return lambda: pl.semaphore_wait(barrier, len(partners))


def gather_kernel(q, k, v, qh, kv, own_sem, s_send, s_recv, g_send, g_recv, t_send, t_recv):
    me = Place()
    left, right = lax.rem(me.r + 3, 4), lax.rem(me.r + 1, 4)
    wait_all = greet(
        [me.at_member(me.member(i)) for i in (1, 2, 3)]
        + [me.at_ring(left), me.at_ring(right), me.at_twin()]
    )
    mine = head_columns(me.m)
    own = [
        pltpu.make_async_copy(k.at[:, mine], kv.at[me.r, me.m, 0], own_sem.at[0]),
        pltpu.make_async_copy(v.at[:, mine], kv.at[me.r, me.m, 1], own_sem.at[1]),
        pltpu.make_async_copy(q.at[:, mine], qh.at[me.pair, me.m], own_sem.at[2]),
    ]
    for copy in own:
        copy.start()
    wait_all()

    sends = []

    def start(copy):
        copy.start()
        sends.append(copy)

    def spread(i, a):
        to = me.member(i)
        dst = qh.at[me.pair, me.m] if a == 2 else kv.at[me.r, me.m, a]
        return remote(
            (k, v, q)[a].at[:, head_columns(to)], dst,
            s_send.at[i - 1, a], s_recv.at[i - 1, a], me.at_member(to),
        )

    def ring(i, j, rel, origin, to):
        slot = kv.at[origin, me.member(i), j]
        return remote(slot, slot, g_send.at[i, j, rel], g_recv.at[i, j, rel], me.at_ring(to))

    def twin(i):
        slot = qh.at[me.pair, me.member(i)]
        return remote(slot, slot, t_send.at[i], t_recv.at[i], me.at_twin())

    def arrived(i, j, rel):
        ring(i, j, rel, me.r, right).wait_recv()

    for a in (0, 1, 2):
        for i in (1, 2, 3):
            start(spread(i, a))
    for i in range(5):
        if i < 4:
            for j in (0, 1):
                if i == 0:
                    own[j].wait()
                else:
                    spread(i, j).wait_recv()
                start(ring(i, j, 0, me.r, right))
                start(ring(i, j, 1, me.r, left))
        if i >= 1:
            arrived(i - 1, 0, 0)
            start(ring(i - 1, 0, 2, left, right))
            arrived(i - 1, 1, 1)
            start(ring(i - 1, 1, 2, right, left))
    own[2].wait()
    start(twin(0))
    for i in (1, 2, 3):
        spread(i, 2).wait_recv()
        start(twin(i))
    for i in range(4):
        arrived(i, 0, 1)
        arrived(i, 1, 0)
        arrived(i, 0, 2)
        arrived(i, 1, 2)
        twin(i).wait_recv()
    for copy in sends:
        copy.wait_send()


def gather(q, k, v):
    rows = q.shape[0]
    anywhere, near = pl.BlockSpec(memory_space=pltpu.HBM), pl.BlockSpec(memory_space=pltpu.VMEM)
    dma = pltpu.SemaphoreType.DMA
    return pl.pallas_call(
        gather_kernel,
        name="spread_and_gather",
        out_shape=(
            jax.ShapeDtypeStruct((2, 4, rows, HEAD), q.dtype),
            jax.ShapeDtypeStruct((4, 4, 2, rows, HEAD), q.dtype),
        ),
        in_specs=[anywhere] * 3,
        out_specs=(near, near),
        scratch_shapes=[
            dma((3,)), dma((3, 3)), dma((3, 3)), dma((4, 2, 3)), dma((4, 2, 3)), dma((4,)), dma((4,)),
        ],
        compiler_params=pltpu.CompilerParams(
            collective_id=0, has_side_effects=True, vmem_limit_bytes=VMEM_BYTES
        ),
    )(q, k, v)


def attend_kernel(
    far_lengths, far_layout, q, kv, out, logs,
    lengths, layout, start, where_is, doc_at, work, count, lows, top, total, summed, table_sem,
):
    me = Place()
    tables = [
        pltpu.make_async_copy(far_lengths, lengths, table_sem.at[0]),
        pltpu.make_async_copy(far_layout, layout, table_sem.at[1]),
    ]
    for copy in tables:
        copy.start()
    top[...] = jnp.full(top.shape, LEAST, jnp.float32)
    total[...] = jnp.zeros(total.shape, jnp.float32)
    for copy in tables:
        copy.wait()
    blocks, docs = layout.shape[0], lengths.shape[0]
    half = q.shape[2] // 2
    spare = 16

    def place(b, _):
        where_is[layout[b]] = b
        return 0

    lax.fori_loop(0, blocks, place, 0)

    def walk(j, at):
        start[j] = at
        end = at + lengths[j]

        def mark(b, _):
            doc_at[b] = j
            return 0

        lax.fori_loop(lax.div(at + half - 1, half), lax.div(end + half - 1, half), mark, 0)
        return end

    start[docs] = lax.fori_loop(0, docs, walk, 0)
    for n in range(STREAMS):
        count[n] = 0

    def query_block(u):
        p, y = member_place(lax.div(u, 8), lax.rem(lax.div(u, 2), 4))
        return layout[ctx_of(me.core, p, me.r, y) * 2 + lax.rem(u, 2)]

    def plan(u, _):
        block = query_block(u)
        base = block * half
        first_doc = doc_at[block]
        q_pos = base + lax.broadcasted_iota(jnp.int32, (1, half), 1)

        def doc_start(state):
            j, low = state
            at = start[j]
            return j + 1, jnp.where(q_pos >= at, at, low)

        _, low = lax.while_loop(
            lambda state: start[state[0]] < base + half,
            doc_start,
            (first_doc + 1, jnp.full((1, half), start[first_doc], jnp.int32)),
        )
        lows[u] = low
        summed[u] = jnp.zeros((HEAD, half), jnp.float32)
        stream = jnp.int32(0)
        for n in range(1, STREAMS):
            stream = jnp.where(count[n] < count[stream], n, stream)

        def add(key_block, filled):
            at = where_is[key_block]
            p, r, y = split_ctx(lax.div(at, 2), me.core)
            slot = r * 8 + (y * 2 + pair_bit(p)) * 2 + lax.rem(at, 2)
            work[stream, filled] = (u * blocks + key_block) * 32 + slot
            return filled + jnp.where(lax.div(p, 2) == me.pair, 1, 0)

        count[stream] = lax.fori_loop(
            lax.div(start[first_doc], half), block + 1, add, count[stream]
        )
        return 0

    lax.fori_loop(0, 16, plan, 0)
    steps = count[0]
    for n in range(1, STREAMS):
        steps = jnp.maximum(steps, count[n])
    for n in range(STREAMS):

        def fill(t, _):
            work[n, t] = (spare + n) * blocks * 32
            return 0

        lax.fori_loop(count[n], steps, fill, 0)

    def step(t, _):
        todo = []
        for n in range(STREAMS):
            code = work[n, t]
            slot = lax.rem(code, 32)
            key_block = lax.rem(lax.div(code, 32), blocks)
            u = lax.div(code, 32 * blocks)
            real = jnp.minimum(u, spare - 1)
            q_rows = pl.ds(pl.multiple_of(lax.rem(real, 2) * half, half), half)
            k_rows = pl.ds(pl.multiple_of(lax.rem(slot, 2) * half, half), half)
            r_k, m_k = lax.div(slot, 8), lax.rem(lax.div(slot, 2), 4)
            query = q[lax.div(real, 8), lax.rem(lax.div(real, 2), 4), q_rows, :]
            key, value = kv[r_k, m_k, 0, k_rows, :], kv[r_k, m_k, 1, k_rows, :]
            q_pos = query_block(real) * half + lax.broadcasted_iota(jnp.int32, (1, half), 1)
            todo.append((u, key_block, query, key, value, q_pos, lows[real]))
        scores = [
            lax.dot_general(key, query, (((1,), (1,)), ((), ())), preferred_element_type=jnp.float32)
            for _, _, query, key, _, _, _ in todo
        ]
        for n, (u, key_block, _, _, value, q_pos, low) in enumerate(todo):
            k_pos = key_block * half + lax.broadcasted_iota(jnp.int32, (half, half), 0)
            masked = jnp.where((k_pos >= low) & (k_pos <= q_pos), scores[n], -1e30)
            old = top[u]
            new = jnp.maximum(old, jnp.max(masked, axis=0, keepdims=True))
            weights = jnp.exp2((masked - new) * (SCALE * LOG2E))
            factor = jnp.exp2((old - new) * (SCALE * LOG2E))
            top[u] = new
            total[u] = total[u] * factor + jnp.sum(weights, axis=0, keepdims=True)
            summed[u] = summed[u] * factor + lax.dot_general(
                value,
                weights.astype(jnp.bfloat16),
                (((0,), (0,)), ((), ())),
                preferred_element_type=jnp.float32,
            )
        return 0

    lax.fori_loop(0, steps, step, 0)

    def finish(u, _):
        at = (lax.div(u, 8), lax.rem(lax.div(u, 2), 4))
        rows = pl.ds(pl.multiple_of(lax.rem(u, 2) * half, half), half)
        some = total[u] > 0.0
        safe = jnp.where(some, total[u], 1.0)
        out[at[0], at[1], :, rows] = (summed[u] * (1.0 / safe)).astype(out.dtype)
        logs[at[0], at[1], :, rows] = jnp.where(some, top[u] * SCALE + jnp.log(safe), -1e30)
        return 0

    lax.fori_loop(0, 16, finish, 0)


def attend(lengths, layout, q, kv):
    rows, blocks = q.shape[2], layout.shape[0]
    half = rows // 2
    far, near = pl.BlockSpec(memory_space=pltpu.HBM), pl.BlockSpec(memory_space=pltpu.VMEM)
    return pl.pallas_call(
        attend_kernel,
        name="attend",
        out_shape=(
            jax.ShapeDtypeStruct((2, 4, HEAD, rows), q.dtype),
            jax.ShapeDtypeStruct((2, 4, 1, rows), jnp.float32),
        ),
        in_specs=[far, far, near, near],
        out_specs=(near, near),
        scratch_shapes=[
            pltpu.SMEM(lengths.shape, jnp.int32),
            pltpu.SMEM(layout.shape, jnp.int32),
            pltpu.SMEM((lengths.shape[0] + 1,), jnp.int32),
            pltpu.SMEM((blocks,), jnp.int32),
            pltpu.SMEM((blocks,), jnp.int32),
            pltpu.SMEM((STREAMS, 16 * blocks + 1), jnp.int32),
            pltpu.SMEM((STREAMS,), jnp.int32),
            pltpu.VMEM((16, 1, half), jnp.int32),
            pltpu.VMEM((16 + STREAMS, 1, half), jnp.float32),
            pltpu.VMEM((16 + STREAMS, 1, half), jnp.float32),
            pltpu.VMEM((16 + STREAMS, HEAD, half), jnp.float32),
            pltpu.SemaphoreType.DMA((2,)),
        ],
        compiler_params=pltpu.CompilerParams(vmem_limit_bytes=VMEM_BYTES),
    )(lengths, layout, q, kv)


CHUNKS = 4


def project_kernel(
    o, logs, w, mixed, log_out,
    o_in, lo_in, merged, merged_logs, att, logs_in, own_sum, c_out, c_in, y_out, y_in,
    b_send, b_recv, lb_sem, a_send, a_recv, l_send, l_recv, c_send, c_recv, y_send, y_recv,
):
    me = Place()
    rows, columns = mixed.shape
    part = rows // CHUNKS
    high, core = me.high, me.core
    targets = ((1 - high) * 2 + 1 - core, (1 - high) * 2 + core, high * 2 + 1 - core, me.tp)
    mate, across = (me.ctx, targets[2]), (me.ctx, targets[1])
    greet(
        [me.at_member(me.member(i)) for i in (1, 2, 3)] + [me.at_twin(), mate, across]
    )()
    sends = []

    def start(copy):
        copy.start()
        sends.append(copy)

    order = (3, 1, 2, 0)

    def to_twin(i):
        m = me.member(i)
        return remote(o.at[1 - me.pair, m], o_in.at[m], b_send.at[i], b_recv.at[i], me.at_twin())

    def to_owner(i):
        m = me.member(i)
        return remote(
            merged.at[i - 1], att.at[:, head_columns(me.m)],
            a_send.at[i - 1], a_recv.at[i - 1], me.at_member(m),
        )

    def log_to_owner(i):
        m = me.member(i)
        return remote(
            merged_logs.at[i - 1], logs_in.at[me.m],
            l_send.at[i - 1], l_recv.at[i - 1], me.at_member(m),
        )

    twin_logs = remote(logs.at[1 - me.pair], lo_in, lb_sem.at[0], lb_sem.at[1], me.at_twin())
    start(twin_logs)
    for i in order:
        start(to_twin(i))
    twin_logs.wait_recv()
    for i in order:
        m = me.member(i)
        one, two = logs[me.pair, m], lo_in[m]
        most = jnp.maximum(one, two)
        e_one, e_two = jnp.exp(one - most), jnp.exp(two - most)
        both = e_one + e_two
        final = most + jnp.log(both)
        share = 1.0 / both
        to_twin(i).wait_recv()
        whole = o[me.pair, m].astype(jnp.float32) * (e_one * share) + o_in[m].astype(
            jnp.float32
        ) * (e_two * share)
        turned = whole.T.astype(jnp.bfloat16)
        if i == 0:
            att[:, head_columns(me.m)] = turned
            logs_in[me.m] = final
        else:
            merged[i - 1] = turned
            merged_logs[i - 1] = final
            start(to_owner(i))
            start(log_to_owner(i))
    for i in (1, 2, 3):
        to_owner(i).wait_recv()

    def chunk(c):
        return pl.ds(c * part, part)

    def product(c, n):
        at = pl.ds(pl.multiple_of(targets[n] * columns, columns), columns)
        return jnp.dot(att[chunk(c), :], w[:, at], preferred_element_type=jnp.float32)

    def to_mate(c, n):
        return remote(
            c_out.at[n, chunk(c)], c_in.at[n, chunk(c)], c_send.at[n, c], c_recv.at[n, c], mate
        )

    def to_across(c):
        return remote(y_out.at[chunk(c)], y_in.at[chunk(c)], y_send.at[c], y_recv.at[c], across)

    def give(c, n):
        c_out[n, chunk(c), :] = product(c, 2 * n).astype(jnp.bfloat16)
        start(to_mate(c, n))

    def pass_on(c):
        mine = product(c, 1)
        to_mate(c, 0).wait_recv()
        y_out[chunk(c), :] = (mine + c_in[0, chunk(c), :].astype(jnp.float32)).astype(jnp.bfloat16)
        start(to_across(c))

    give(0, 0)
    for c in range(CHUNKS):
        if c + 1 < CHUNKS:
            give(c + 1, 0)
        pass_on(c)
    for c in range(CHUNKS):
        give(c, 1)
    for c in range(CHUNKS):
        mine = product(c, 3)
        to_mate(c, 1).wait_recv()
        own_sum[chunk(c), :] = mine + c_in[1, chunk(c), :].astype(jnp.float32)
    for i in (1, 2, 3):
        log_to_owner(i).wait_recv()
    for h in range(4):
        log_out[h : h + 1, :] = logs_in[h]
    for c in range(CHUNKS):
        to_across(c).wait_recv()
        mixed[chunk(c), :] = (own_sum[chunk(c), :] + y_in[chunk(c), :].astype(jnp.float32)).astype(
            jnp.bfloat16
        )
    for copy in sends:
        copy.wait_send()


def project(o, logs, w):
    rows, depth, columns = o.shape[3], w.shape[0], w.shape[1] // 4
    near = pl.BlockSpec(memory_space=pltpu.VMEM)
    dma = pltpu.SemaphoreType.DMA
    return pl.pallas_call(
        project_kernel,
        name="return_and_project",
        out_shape=(
            jax.ShapeDtypeStruct((rows, columns), jnp.bfloat16),
            jax.ShapeDtypeStruct((4, rows), jnp.float32),
        ),
        in_specs=[near, near, near],
        out_specs=(near, near),
        scratch_shapes=[
            pltpu.VMEM((4, HEAD, rows), jnp.bfloat16),
            pltpu.VMEM((4, 1, rows), jnp.float32),
            pltpu.VMEM((3, rows, HEAD), jnp.bfloat16),
            pltpu.VMEM((3, 1, rows), jnp.float32),
            pltpu.VMEM((rows, depth), jnp.bfloat16),
            pltpu.VMEM((4, 1, rows), jnp.float32),
            pltpu.VMEM((rows, columns), jnp.float32),
            pltpu.VMEM((2, rows, columns), jnp.bfloat16),
            pltpu.VMEM((2, rows, columns), jnp.bfloat16),
            pltpu.VMEM((rows, columns), jnp.bfloat16),
            pltpu.VMEM((rows, columns), jnp.bfloat16),
            dma((4,)), dma((4,)), dma((2,)), dma((3,)), dma((3,)), dma((3,)), dma((3,)),
            dma((2, CHUNKS)), dma((2, CHUNKS)), dma((CHUNKS,)), dma((CHUNKS,)),
        ],
        compiler_params=pltpu.CompilerParams(
            collective_id=1, has_side_effects=True, vmem_limit_bytes=VMEM_BYTES
        ),
    )(o, logs, w)


def local(queries, keys, values, out_weight, doc_lengths, layout):
    qh, kv = gather(queries, keys, values)
    o, logs = attend(doc_lengths, layout, qh, kv)
    return project(o, logs, out_weight)


def solution(mesh):
    placed = (P("ctx", "tp"), P("ctx", "tp"), P("ctx", "tp"), P("tp", None), P(), P())
    return jax.shard_map(
        local,
        mesh=mesh,
        in_specs=placed,
        out_specs=(P("ctx", "tp"), P("tp", "ctx")),
        check_vma=False,
    )
```

```python
import math

import jax
import jax.numpy as jnp
from jax import lax
from jax.experimental import pallas as pl
from jax.experimental.pallas import tpu as pltpu
from jax.sharding import PartitionSpec as P

HEAD = 128
MESH = pl.DeviceIdType.MESH
SCALE = 1.0 / math.sqrt(HEAD)
LOG2E = math.log2(math.e)
STREAMS = 4
LEAST = -1e29
PART = 128
VMEM_BYTES = 40 * 1024 * 1024


def ctx_of(core, p, r, y):
    return p * (8 - 6 * core) + r * (2 + 6 * core) + y


def split_ctx(ctx, core):
    z, x, y = lax.div(ctx, 8), lax.rem(lax.div(ctx, 2), 4), lax.rem(ctx, 2)
    return z * (1 - core) + x * core, x * (1 - core) + z * core, y


def pair_bit(p):
    return lax.rem(lax.div(p + 1, 2), 2)


def member_place(pair, m):
    bit = lax.rem(m, 2)
    return bit + pair * (3 - 2 * bit), lax.div(m, 2)


class Place:
    def __init__(self):
        self.ctx, self.tp = lax.axis_index("ctx"), lax.axis_index("tp")
        self.core, self.high = lax.rem(self.tp, 2), lax.div(self.tp, 2)
        self.p, self.r, self.y = split_ctx(self.ctx, self.core)
        self.pair, self.bit = lax.div(self.p, 2), pair_bit(self.p)
        self.m = self.y * 2 + self.bit
        self.mate = self.high * 2 + 1 - self.core
        self.across = (1 - self.high) * 2 + self.core
        self.diagonal = (1 - self.high) * 2 + 1 - self.core

    def member(self, i):
        bit = 1 - self.bit if i % 2 else self.bit
        y = 1 - self.y if i // 2 else self.y
        return y * 2 + bit

    def at_member(self, m):
        p, y = member_place(self.pair, m)
        return (ctx_of(self.core, p, self.r, y), self.tp)

    def at_ring(self, r):
        return (ctx_of(self.core, self.p, r, self.y), self.tp)

    def at_tp(self, tp):
        return (self.ctx, tp)

    def at_twin(self):
        return (ctx_of(self.core, 3 - self.p, self.r, self.y), self.tp)


def head_columns(m):
    return pl.ds(pl.multiple_of(m * HEAD, HEAD), HEAD)


def remote(src, dst, send_sem, recv_sem, to):
    return pltpu.make_async_remote_copy(
        src_ref=src, dst_ref=dst, send_sem=send_sem, recv_sem=recv_sem,
        device_id=to, device_id_type=MESH,
    )


def greet(partners):
    barrier = pltpu.get_barrier_semaphore()
    for partner in partners:
        pl.semaphore_signal(barrier, inc=1, device_id=partner, device_id_type=MESH)
    return lambda: pl.semaphore_wait(barrier, len(partners))


def gather_kernel(
    q, k, v, w, qh, kv, w_near, w_far,
    own_sem, s_send, s_recv, g_send, g_recv, t_send, t_recv, w_send, w_recv,
):
    me = Place()
    left, right = lax.rem(me.r + 3, 4), lax.rem(me.r + 1, 4)
    wait_all = greet(
        [me.at_member(me.member(i)) for i in (1, 2, 3)]
        + [me.at_ring(left), me.at_ring(right), me.at_twin(), me.at_tp(me.mate)]
        + [me.at_tp(me.across), me.at_tp(me.diagonal)]
    )
    mine = head_columns(me.m)
    columns = w_near.shape[2]
    quarter = w_far.shape[1]

    def weight_columns(tp):
        return pl.ds(pl.multiple_of(tp * columns, columns), columns)

    own = [
        pltpu.make_async_copy(k.at[:, mine], kv.at[me.r, me.m, 0], own_sem.at[0]),
        pltpu.make_async_copy(v.at[:, mine], kv.at[me.r, me.m, 1], own_sem.at[1]),
        pltpu.make_async_copy(q.at[:, mine], qh.at[me.pair, me.m], own_sem.at[2]),
        pltpu.make_async_copy(w.at[:, weight_columns(me.tp)], w_near.at[0], own_sem.at[3]),
    ]
    for copy in own:
        copy.start()
    wait_all()

    sends = []

    def start(copy):
        copy.start()
        sends.append(copy)

    def spread(i, a):
        to = me.member(i)
        dst = qh.at[me.pair, me.m] if a == 2 else kv.at[me.r, me.m, a]
        return remote(
            (k, v, q)[a].at[:, head_columns(to)], dst,
            s_send.at[i - 1, a], s_recv.at[i - 1, a], me.at_member(to),
        )

    def ring(i, j, rel, origin, to):
        slot = kv.at[origin, me.member(i), j]
        return remote(slot, slot, g_send.at[i, j, rel], g_recv.at[i, j, rel], me.at_ring(to))

    def twin(i):
        slot = qh.at[me.pair, me.member(i)]
        return remote(slot, slot, t_send.at[i], t_recv.at[i], me.at_twin())

    def arrived(i, j, rel):
        ring(i, j, rel, me.r, right).wait_recv()

    def weights_across(n):
        to = (me.across, me.diagonal)[n]
        place = (me.r, me.p)[n]
        rows = pl.ds(pl.multiple_of(place * quarter, quarter), quarter)
        return remote(
            w.at[rows, weight_columns(to)], w_far.at[me.core],
            w_send.at[n], w_recv.at[n], me.at_tp(to),
        )

    weights_to_mate = remote(
        w.at[:, weight_columns(me.mate)], w_near.at[1], w_send.at[2], w_recv.at[2], me.at_tp(me.mate)
    )
    for a in (0, 1, 2):
        for i in (1, 2, 3):
            start(spread(i, a))
    for i in range(5):
        if i < 4:
            for j in (0, 1):
                if i == 0:
                    own[j].wait()
                else:
                    spread(i, j).wait_recv()
                start(ring(i, j, 0, me.r, right))
                start(ring(i, j, 1, me.r, left))
        if i >= 1:
            arrived(i - 1, 0, 0)
            start(ring(i - 1, 0, 2, left, right))
            arrived(i - 1, 1, 1)
            start(ring(i - 1, 1, 2, right, left))
        if i == 3:
            start(weights_across(0))
            start(weights_across(1))
            start(weights_to_mate)
    own[2].wait()
    own[3].wait()
    start(twin(0))
    for i in (1, 2, 3):
        spread(i, 2).wait_recv()
        start(twin(i))
    for i in range(4):
        arrived(i, 0, 1)
        arrived(i, 1, 0)
        arrived(i, 0, 2)
        arrived(i, 1, 2)
        twin(i).wait_recv()
    weights_across(0).wait_recv()
    weights_across(1).wait_recv()
    weights_to_mate.wait_recv()
    for copy in sends:
        copy.wait_send()


def gather(q, k, v, w):
    rows, depth, columns = q.shape[0], w.shape[0], w.shape[1] // 4
    anywhere, near = pl.BlockSpec(memory_space=pltpu.HBM), pl.BlockSpec(memory_space=pltpu.VMEM)
    dma = pltpu.SemaphoreType.DMA
    return pl.pallas_call(
        gather_kernel,
        name="spread_and_gather",
        out_shape=(
            jax.ShapeDtypeStruct((2, 4, rows, HEAD), q.dtype),
            jax.ShapeDtypeStruct((4, 4, 2, rows, HEAD), q.dtype),
            jax.ShapeDtypeStruct((2, depth, columns), w.dtype),
            jax.ShapeDtypeStruct((2, depth // 4, columns), w.dtype),
        ),
        in_specs=[anywhere] * 4,
        out_specs=(near,) * 4,
        scratch_shapes=[
            dma((4,)), dma((3, 3)), dma((3, 3)), dma((4, 2, 3)), dma((4, 2, 3)), dma((4,)), dma((4,)),
            dma((3,)), dma((3,)),
        ],
        compiler_params=pltpu.CompilerParams(
            collective_id=0, has_side_effects=True, vmem_limit_bytes=VMEM_BYTES
        ),
    )(q, k, v, w)


def attend_kernel(
    far_lengths, far_layout, q, kv, out, logs,
    lengths, layout, start, where_is, doc_at, work, count, lows, top, total, summed, table_sem,
):
    me = Place()
    tables = [
        pltpu.make_async_copy(far_lengths, lengths, table_sem.at[0]),
        pltpu.make_async_copy(far_layout, layout, table_sem.at[1]),
    ]
    for copy in tables:
        copy.start()
    top[...] = jnp.full(top.shape, LEAST, jnp.float32)
    total[...] = jnp.zeros(total.shape, jnp.float32)
    for copy in tables:
        copy.wait()
    blocks, docs = layout.shape[0], lengths.shape[0]
    half = q.shape[2] // 2
    spare = 16

    def place(b, _):
        where_is[layout[b]] = b
        return 0

    lax.fori_loop(0, blocks, place, 0)

    def walk(j, at):
        start[j] = at
        end = at + lengths[j]

        def mark(b, _):
            doc_at[b] = j
            return 0

        lax.fori_loop(lax.div(at + half - 1, half), lax.div(end + half - 1, half), mark, 0)
        return end

    start[docs] = lax.fori_loop(0, docs, walk, 0)
    for n in range(STREAMS):
        count[n] = 0

    def query_block(u):
        p, y = member_place(lax.div(u, 8), lax.rem(lax.div(u, 2), 4))
        return layout[ctx_of(me.core, p, me.r, y) * 2 + lax.rem(u, 2)]

    def plan(u, _):
        block = query_block(u)
        base = block * half
        first_doc = doc_at[block]
        q_pos = base + lax.broadcasted_iota(jnp.int32, (1, half), 1)

        def doc_start(state):
            j, low = state
            at = start[j]
            return j + 1, jnp.where(q_pos >= at, at, low)

        _, low = lax.while_loop(
            lambda state: start[state[0]] < base + half,
            doc_start,
            (first_doc + 1, jnp.full((1, half), start[first_doc], jnp.int32)),
        )
        lows[u] = low
        summed[u] = jnp.zeros((HEAD, half), jnp.float32)
        stream = jnp.int32(0)
        for n in range(1, STREAMS):
            stream = jnp.where(count[n] < count[stream], n, stream)

        def add(key_block, filled):
            at = where_is[key_block]
            p, r, y = split_ctx(lax.div(at, 2), me.core)
            slot = r * 8 + (y * 2 + pair_bit(p)) * 2 + lax.rem(at, 2)
            work[stream, filled] = (u * blocks + key_block) * 32 + slot
            return filled + jnp.where(lax.div(p, 2) == me.pair, 1, 0)

        count[stream] = lax.fori_loop(
            lax.div(start[first_doc], half), block + 1, add, count[stream]
        )
        return 0

    lax.fori_loop(0, 16, plan, 0)
    steps = count[0]
    for n in range(1, STREAMS):
        steps = jnp.maximum(steps, count[n])
    for n in range(STREAMS):

        def fill(t, _):
            work[n, t] = (spare + n) * blocks * 32
            return 0

        lax.fori_loop(count[n], steps, fill, 0)

    def step(t, _):
        todo = []
        for n in range(STREAMS):
            code = work[n, t]
            slot = lax.rem(code, 32)
            key_block = lax.rem(lax.div(code, 32), blocks)
            u = lax.div(code, 32 * blocks)
            real = jnp.minimum(u, spare - 1)
            q_rows = pl.ds(pl.multiple_of(lax.rem(real, 2) * half, half), half)
            k_rows = pl.ds(pl.multiple_of(lax.rem(slot, 2) * half, half), half)
            r_k, m_k = lax.div(slot, 8), lax.rem(lax.div(slot, 2), 4)
            query = q[lax.div(real, 8), lax.rem(lax.div(real, 2), 4), q_rows, :]
            key, value = kv[r_k, m_k, 0, k_rows, :], kv[r_k, m_k, 1, k_rows, :]
            q_pos = query_block(real) * half + lax.broadcasted_iota(jnp.int32, (1, half), 1)
            todo.append((u, key_block, query, key, value, q_pos, lows[real]))
        scores = [
            lax.dot_general(key, query, (((1,), (1,)), ((), ())), preferred_element_type=jnp.float32)
            for _, _, query, key, _, _, _ in todo
        ]
        for n, (u, key_block, _, _, value, q_pos, low) in enumerate(todo):
            k_pos = key_block * half + lax.broadcasted_iota(jnp.int32, (half, half), 0)
            masked = jnp.where((k_pos >= low) & (k_pos <= q_pos), scores[n], -1e30)
            old = top[u]
            new = jnp.maximum(old, jnp.max(masked, axis=0, keepdims=True))
            weights = jnp.exp2((masked - new) * (SCALE * LOG2E))
            factor = jnp.exp2((old - new) * (SCALE * LOG2E))
            top[u] = new
            total[u] = total[u] * factor + jnp.sum(weights, axis=0, keepdims=True)
            summed[u] = summed[u] * factor + lax.dot_general(
                value,
                weights.astype(jnp.bfloat16),
                (((0,), (0,)), ((), ())),
                preferred_element_type=jnp.float32,
            )
        return 0

    lax.fori_loop(0, steps, step, 0)

    def finish(u, _):
        at = (lax.div(u, 8), lax.rem(lax.div(u, 2), 4))
        rows = pl.ds(pl.multiple_of(lax.rem(u, 2) * half, half), half)
        some = total[u] > 0.0
        safe = jnp.where(some, total[u], 1.0)
        attended = (summed[u] * (1.0 / safe)).astype(out.dtype)
        for e in range(half // PART):
            chunk = lax.rem(u, 2) * (half // PART) + e
            out[at[0], at[1], chunk] = attended[:, e * PART : (e + 1) * PART]
        logs[at[0], at[1], :, rows] = jnp.where(some, top[u] * SCALE + jnp.log(safe), -1e30)
        return 0

    lax.fori_loop(0, 16, finish, 0)


def attend(lengths, layout, q, kv):
    rows, blocks = q.shape[2], layout.shape[0]
    half = rows // 2
    far, near = pl.BlockSpec(memory_space=pltpu.HBM), pl.BlockSpec(memory_space=pltpu.VMEM)
    return pl.pallas_call(
        attend_kernel,
        name="attend",
        out_shape=(
            jax.ShapeDtypeStruct((2, 4, rows // PART, HEAD, PART), q.dtype),
            jax.ShapeDtypeStruct((2, 4, 1, rows), jnp.float32),
        ),
        in_specs=[far, far, near, near],
        out_specs=(near, near),
        scratch_shapes=[
            pltpu.SMEM(lengths.shape, jnp.int32),
            pltpu.SMEM(layout.shape, jnp.int32),
            pltpu.SMEM((lengths.shape[0] + 1,), jnp.int32),
            pltpu.SMEM((blocks,), jnp.int32),
            pltpu.SMEM((blocks,), jnp.int32),
            pltpu.SMEM((STREAMS, 16 * blocks + 1), jnp.int32),
            pltpu.SMEM((STREAMS,), jnp.int32),
            pltpu.VMEM((16, 1, half), jnp.int32),
            pltpu.VMEM((16 + STREAMS, 1, half), jnp.float32),
            pltpu.VMEM((16 + STREAMS, 1, half), jnp.float32),
            pltpu.VMEM((16 + STREAMS, HEAD, half), jnp.float32),
            pltpu.SemaphoreType.DMA((2,)),
        ],
        compiler_params=pltpu.CompilerParams(vmem_limit_bytes=VMEM_BYTES),
    )(lengths, layout, q, kv)


def project_kernel(
    o, logs, w_near, w_quarter, mixed, log_out,
    o_in, lo_in, merged, merged_logs, att, att_in, logs_in, w_far, total,
    own_sem, b_send, b_recv, lb_sem, a_send, a_recv, l_send, l_recv, x_send, x_recv, w_send, w_recv,
):
    me = Place()
    chunks = o.shape[2]
    left, right = lax.rem(me.r + 3, 4), lax.rem(me.r + 1, 4)
    wait_all = greet(
        [me.at_member(me.member(i)) for i in (1, 2, 3)]
        + [me.at_ring(left), me.at_ring(right), me.at_twin()]
        + [me.at_tp(me.mate), me.at_tp(me.across)]
    )
    own = [
        pltpu.make_async_copy(w_quarter.at[n], w_far.at[n, me.r], own_sem.at[n]) for n in (0, 1)
    ]
    for copy in own:
        copy.start()
    wait_all()
    sends = []

    def start(copy):
        copy.start()
        sends.append(copy)

    order = (3, 1, 2, 0)

    def to_twin(i, c):
        m = me.member(i)
        return remote(
            o.at[1 - me.pair, m, c], o_in.at[m, c], b_send.at[i, c], b_recv.at[i, c], me.at_twin()
        )

    def to_owner(i, c):
        return remote(
            merged.at[i - 1, c], att.at[c, :, head_columns(me.m)],
            a_send.at[i - 1, c], a_recv.at[i - 1, c], me.at_member(me.member(i)),
        )

    def log_to_owner(i):
        return remote(
            merged_logs.at[i], logs_in.at[me.m],
            l_send.at[i - 1], l_recv.at[i - 1], me.at_member(me.member(i)),
        )

    def pass_att(n, c):
        src = att_in.at[0, c] if n == 2 else att.at[c]
        to = me.across if n == 0 else me.mate
        return remote(src, att_in.at[n, c], x_send.at[n, c], x_recv.at[n, c], me.at_tp(to))

    def weights(n, rel, origin, to):
        slot = w_far.at[n, origin]
        return remote(slot, slot, w_send.at[n, rel], w_recv.at[n, rel], me.at_ring(to))

    def weights_arrived(n, rel):
        weights(n, rel, me.r, right).wait_recv()

    twin_logs = remote(logs.at[1 - me.pair], lo_in, lb_sem.at[0], lb_sem.at[1], me.at_twin())
    start(twin_logs)
    for c in range(chunks):
        for i in order:
            start(to_twin(i, c))
    twin_logs.wait_recv()
    shares = []
    for i in range(4):
        m = me.member(i)
        one, two = logs[me.pair, m], lo_in[m]
        most = jnp.maximum(one, two)
        e_one, e_two = jnp.exp(one - most), jnp.exp(two - most)
        both = e_one + e_two
        final = most + jnp.log(both)
        share = 1.0 / both
        shares.append((e_one * share, e_two * share))
        if i == 0:
            logs_in[me.m] = final
        else:
            merged_logs[i] = final
            start(log_to_owner(i))

    def merge(c):
        for i in order:
            m = me.member(i)
            lanes = slice(c * PART, (c + 1) * PART)
            to_twin(i, c).wait_recv()
            whole = (
                o[me.pair, m, c].astype(jnp.float32) * shares[i][0][:, lanes]
                + o_in[m, c].astype(jnp.float32) * shares[i][1][:, lanes]
            )
            turned = whole.T.astype(jnp.bfloat16)
            if i == 0:
                att[c, :, head_columns(me.m)] = turned
            else:
                merged[i - 1, c] = turned
                start(to_owner(i, c))

    def share_out(c):
        for i in (1, 2, 3):
            to_owner(i, c).wait_recv()
        start(pass_att(0, c))
        start(pass_att(1, c))
        total[c] = jnp.dot(att[c], w_near[0], preferred_element_type=jnp.float32)

    def far_weights(n):
        return w_far[n].reshape(w_near.shape[1:])

    def cross(c):
        pass_att(1, c).wait_recv()
        total[c] += jnp.dot(att_in[1, c], w_near[1], preferred_element_type=jnp.float32)
        pass_att(0, c).wait_recv()
        start(pass_att(2, c))

    def finish(c):
        both = total[c] + jnp.dot(
            att_in[0, c], far_weights(me.core), preferred_element_type=jnp.float32
        )
        pass_att(2, c).wait_recv()
        both += jnp.dot(
            att_in[2, c], far_weights(1 - me.core), preferred_element_type=jnp.float32
        )
        mixed[c * PART : (c + 1) * PART, :] = both.astype(mixed.dtype)

    for t in range(chunks + 3):
        if t < chunks:
            merge(t)
        if t == 0:
            for n in (0, 1):
                own[n].wait()
                start(weights(n, 0, me.r, right))
                start(weights(n, 1, me.r, left))
        if 0 <= t - 1 < chunks:
            share_out(t - 1)
        if t == 3:
            weights_arrived(0, 0)
            start(weights(0, 2, left, right))
            weights_arrived(1, 1)
            start(weights(1, 2, right, left))
        if 0 <= t - 2 < chunks:
            cross(t - 2)
        if t == chunks + 1:
            weights_arrived(0, 1)
            weights_arrived(1, 0)
            weights_arrived(0, 2)
            weights_arrived(1, 2)
            for c in range(chunks - 1):
                finish(c)
    finish(chunks - 1)
    for i in (1, 2, 3):
        log_to_owner(i).wait_recv()
    for h in range(4):
        log_out[h : h + 1, :] = logs_in[h]
    for copy in sends:
        copy.wait_send()


def project(o, logs, w_near, w_quarter):
    chunks, depth, columns = o.shape[2], w_near.shape[1], w_near.shape[2]
    rows = chunks * PART
    near = pl.BlockSpec(memory_space=pltpu.VMEM)
    dma = pltpu.SemaphoreType.DMA
    return pl.pallas_call(
        project_kernel,
        name="return_and_project",
        out_shape=(
            jax.ShapeDtypeStruct((rows, columns), jnp.bfloat16),
            jax.ShapeDtypeStruct((4, rows), jnp.float32),
        ),
        in_specs=[near] * 4,
        out_specs=(near, near),
        scratch_shapes=[
            pltpu.VMEM((4, chunks, HEAD, PART), jnp.bfloat16),
            pltpu.VMEM((4, 1, rows), jnp.float32),
            pltpu.VMEM((3, chunks, PART, HEAD), jnp.bfloat16),
            pltpu.VMEM((4, 1, rows), jnp.float32),
            pltpu.VMEM((chunks, PART, depth), jnp.bfloat16),
            pltpu.VMEM((3, chunks, PART, depth), jnp.bfloat16),
            pltpu.VMEM((4, 1, rows), jnp.float32),
            pltpu.VMEM((2, 4, depth // 4, columns), jnp.bfloat16),
            pltpu.VMEM((chunks, PART, columns), jnp.float32),
            dma((2,)), dma((4, chunks)), dma((4, chunks)), dma((2,)), dma((3, chunks)),
            dma((3, chunks)), dma((3,)), dma((3,)), dma((3, chunks)), dma((3, chunks)),
            dma((2, 3)), dma((2, 3)),
        ],
        compiler_params=pltpu.CompilerParams(
            collective_id=1, has_side_effects=True, vmem_limit_bytes=VMEM_BYTES
        ),
    )(o, logs, w_near, w_quarter)


def local(queries, keys, values, out_weight, doc_lengths, layout):
    queries, keys, values, out_weight = (pltpu.with_memory_space_constraint(t, pltpu.HBM) for t in (queries, keys, values, out_weight))
    qh, kv, w_near, w_quarter = gather(queries, keys, values, out_weight)
    o, logs = attend(doc_lengths, layout, qh, kv)
    return project(o, logs, w_near, w_quarter)


def solution(mesh):
    placed = (P("ctx", "tp"), P("ctx", "tp"), P("ctx", "tp"), P("tp", None), P(), P())
    return jax.shard_map(
        local,
        mesh=mesh,
        in_specs=placed,
        out_specs=(P("ctx", "tp"), P("tp", "ctx")),
        check_vma=False,
    )
```

```python
import math

import jax
import jax.numpy as jnp
from jax import lax
from jax.experimental import pallas as pl
from jax.experimental.pallas import tpu as pltpu
from jax.sharding import PartitionSpec as P

HEAD = 128
MESH = pl.DeviceIdType.MESH
SCALE = 1.0 / math.sqrt(HEAD)
LOG2E = math.log2(math.e)
STREAMS = 4
LEAST = -1e29
PART = 128
BLOCKS = 64
VMEM_BYTES = 40 * 1024 * 1024


def ctx_of(core, p, r, y):
    return p * (8 - 6 * core) + r * (2 + 6 * core) + y


def split_ctx(ctx, core):
    z, x, y = lax.div(ctx, 8), lax.rem(lax.div(ctx, 2), 4), lax.rem(ctx, 2)
    return z * (1 - core) + x * core, x * (1 - core) + z * core, y


def pair_bit(p):
    return lax.rem(lax.div(p + 1, 2), 2)


def member_place(pair, m):
    bit = lax.rem(m, 2)
    return bit + pair * (3 - 2 * bit), lax.div(m, 2)


class Place:
    def __init__(self):
        self.ctx, self.tp = lax.axis_index("ctx"), lax.axis_index("tp")
        self.core, self.high = lax.rem(self.tp, 2), lax.div(self.tp, 2)
        self.p, self.r, self.y = split_ctx(self.ctx, self.core)
        self.pair, self.bit = lax.div(self.p, 2), pair_bit(self.p)
        self.m = self.y * 2 + self.bit
        self.mate = self.high * 2 + 1 - self.core
        self.across = (1 - self.high) * 2 + self.core
        self.diagonal = (1 - self.high) * 2 + 1 - self.core

    def member(self, i):
        bit = 1 - self.bit if i % 2 else self.bit
        y = 1 - self.y if i // 2 else self.y
        return y * 2 + bit

    def at_member(self, m):
        p, y = member_place(self.pair, m)
        return (ctx_of(self.core, p, self.r, y), self.tp)

    def at_ring(self, r):
        return (ctx_of(self.core, self.p, r, self.y), self.tp)

    def at_tp(self, tp):
        return (self.ctx, tp)

    def at_twin(self):
        return (ctx_of(self.core, 3 - self.p, self.r, self.y), self.tp)


def head_columns(m):
    return pl.ds(pl.multiple_of(m * HEAD, HEAD), HEAD)


def remote(src, dst, send_sem, recv_sem, to):
    return pltpu.make_async_remote_copy(
        src_ref=src, dst_ref=dst, send_sem=send_sem, recv_sem=recv_sem,
        device_id=to, device_id_type=MESH,
    )


def greet(partners):
    barrier = pltpu.get_barrier_semaphore()
    for partner in partners:
        pl.semaphore_signal(barrier, inc=1, device_id=partner, device_id_type=MESH)
    return lambda: pl.semaphore_wait(barrier, len(partners))


def gather_kernel(
    q, k, v, w, far_lengths, far_layout, qh, kv, w_near, w_far, table, lows,
    lengths, layout, table_sem, own_sem, s_send, s_recv, g_send, g_recv, t_send, t_recv, w_send, w_recv,
):
    me = Place()
    left, right = lax.rem(me.r + 3, 4), lax.rem(me.r + 1, 4)
    wait_all = greet(
        [me.at_member(me.member(i)) for i in (1, 2, 3)]
        + [me.at_ring(left), me.at_ring(right), me.at_twin(), me.at_tp(me.mate)]
        + [me.at_tp(me.across), me.at_tp(me.diagonal)]
    )
    mine = head_columns(me.m)
    columns = w_near.shape[2]
    quarter = w_far.shape[1]

    def weight_columns(tp):
        return pl.ds(pl.multiple_of(tp * columns, columns), columns)

    own = [
        pltpu.make_async_copy(k.at[:, mine], kv.at[me.r, me.m, 0], own_sem.at[0]),
        pltpu.make_async_copy(v.at[:, mine], kv.at[me.r, me.m, 1], own_sem.at[1]),
        pltpu.make_async_copy(q.at[:, mine], qh.at[me.pair, me.m], own_sem.at[2]),
        pltpu.make_async_copy(w.at[:, weight_columns(me.tp)], w_near.at[0], own_sem.at[3]),
    ]
    own += [
        pltpu.make_async_copy(far_lengths, lengths, table_sem.at[0]),
        pltpu.make_async_copy(far_layout, layout, table_sem.at[1]),
    ]
    for copy in own:
        copy.start()
    wait_all()

    sends = []

    def start(copy):
        copy.start()
        sends.append(copy)

    def make_tables():
        own[4].wait()
        own[5].wait()
        half = lows.shape[1]
        lane = lax.broadcasted_iota(jnp.int32, (1, table.shape[1]), 1)
        row = lax.broadcasted_iota(jnp.int32, lows.shape, 0)
        q_pos = lax.broadcasted_iota(jnp.int32, lows.shape, 1)
        for u in range(16):
            p, y = member_place(u // 8, u // 2 % 4)
            block = layout[ctx_of(me.core, p, me.r, y) * 2 + u % 2]
            q_pos += jnp.where(row == u, block * half, 0)

        def place(b, state):
            where_is, held = state
            block = layout[b]
            return jnp.where(lane == block, b, where_is), jnp.where(lane == b, block, held)

        def walk(j, state):
            at, first, low = state
            first = jnp.where(lane * half >= at, at, first)
            low = jnp.where(q_pos >= at, at, low)
            return at + lengths[j], first, low

        none = jnp.zeros_like(lane)
        where_is, held = lax.fori_loop(0, layout.shape[0], place, (none, none))
        _, first, low = lax.fori_loop(
            0, lengths.shape[0], walk, (jnp.int32(0), none, jnp.zeros_like(q_pos))
        )
        table[0:1, :] = where_is
        table[1:2, :] = first
        table[2:3, :] = held
        lows[...] = low

    def spread(i, a):
        to = me.member(i)
        dst = qh.at[me.pair, me.m] if a == 2 else kv.at[me.r, me.m, a]
        return remote(
            (k, v, q)[a].at[:, head_columns(to)], dst,
            s_send.at[i - 1, a], s_recv.at[i - 1, a], me.at_member(to),
        )

    def ring(i, j, rel, origin, to):
        slot = kv.at[origin, me.member(i), j]
        return remote(slot, slot, g_send.at[i, j, rel], g_recv.at[i, j, rel], me.at_ring(to))

    def twin(i):
        slot = qh.at[me.pair, me.member(i)]
        return remote(slot, slot, t_send.at[i], t_recv.at[i], me.at_twin())

    def arrived(i, j, rel):
        ring(i, j, rel, me.r, right).wait_recv()

    def weights_across(n):
        to = (me.across, me.diagonal)[n]
        place = (me.r, me.p)[n]
        rows = pl.ds(pl.multiple_of(place * quarter, quarter), quarter)
        return remote(
            w.at[rows, weight_columns(to)], w_far.at[me.core],
            w_send.at[n], w_recv.at[n], me.at_tp(to),
        )

    weights_to_mate = remote(
        w.at[:, weight_columns(me.mate)], w_near.at[1], w_send.at[2], w_recv.at[2], me.at_tp(me.mate)
    )
    for a in (2, 0, 1):
        for i in (2, 3, 1):
            start(spread(i, a))

    def pass_query(i):
        if i == 0:
            own[2].wait()
        else:
            spread(i, 2).wait_recv()
        start(twin(i))

    def pass_weights():
        start(weights_across(0))
        start(weights_across(1))
        start(weights_to_mate)

    for i in range(5):
        if i < 4:
            for j in (0, 1):
                if i == 0:
                    own[j].wait()
                else:
                    spread(i, j).wait_recv()
                start(ring(i, j, 0, me.r, right))
                start(ring(i, j, 1, me.r, left))
        if i == 0:
            pass_query(0)
            make_tables()
            pass_query(1)
        if i == 1:
            pass_query(2)
            pass_query(3)
        if i == 2:
            pass_weights()
        if i >= 1:
            arrived(i - 1, 0, 0)
            start(ring(i - 1, 0, 2, left, right))
            arrived(i - 1, 1, 1)
            start(ring(i - 1, 1, 2, right, left))
    own[3].wait()
    for i in range(4):
        arrived(i, 0, 1)
        arrived(i, 1, 0)
        arrived(i, 0, 2)
        arrived(i, 1, 2)
        twin(i).wait_recv()
    weights_across(0).wait_recv()
    weights_across(1).wait_recv()
    weights_to_mate.wait_recv()
    for copy in sends:
        copy.wait_send()


def gather(q, k, v, w, lengths, layout):
    rows, depth, columns = q.shape[0], w.shape[0], w.shape[1] // 4
    anywhere, near = pl.BlockSpec(memory_space=pltpu.HBM), pl.BlockSpec(memory_space=pltpu.VMEM)
    dma = pltpu.SemaphoreType.DMA
    return pl.pallas_call(
        gather_kernel,
        name="spread_and_gather",
        out_shape=(
            jax.ShapeDtypeStruct((2, 4, rows, HEAD), q.dtype),
            jax.ShapeDtypeStruct((4, 4, 2, rows, HEAD), q.dtype),
            jax.ShapeDtypeStruct((2, depth, columns), w.dtype),
            jax.ShapeDtypeStruct((2, depth // 4, columns), w.dtype),
            jax.ShapeDtypeStruct((8, 128), jnp.int32),
            jax.ShapeDtypeStruct((16, rows // 2), jnp.int32),
        ),
        in_specs=[anywhere] * 6,
        out_specs=(near,) * 6,
        scratch_shapes=[
            pltpu.SMEM(lengths.shape, jnp.int32),
            pltpu.SMEM(layout.shape, jnp.int32),
            dma((2,)),
            dma((4,)), dma((3, 3)), dma((3, 3)), dma((4, 2, 3)), dma((4, 2, 3)), dma((4,)), dma((4,)),
            dma((3,)), dma((3,)),
        ],
        compiler_params=pltpu.CompilerParams(
            collective_id=0, has_side_effects=True, vmem_limit_bytes=VMEM_BYTES
        ),
    )(q, k, v, w, lengths, layout)


def attend_kernel(
    near_table, lows, q, kv, out, logs, table, work, count, top, total, summed, table_sem
):
    me = Place()
    blocks = BLOCKS
    half = q.shape[2] // 2
    spare = 16
    fetch = pltpu.make_async_copy(near_table, table, table_sem.at[0])
    fetch.start()
    top[...] = jnp.full(top.shape, LEAST, jnp.float32)
    total[...] = jnp.zeros(total.shape, jnp.float32)
    summed[...] = jnp.zeros(summed.shape, jnp.float32)
    for n in range(STREAMS):
        count[n] = 0
    fetch.wait()

    def query_block(u):
        p, y = member_place(lax.div(u, 8), lax.rem(lax.div(u, 2), 4))
        return table[2, ctx_of(me.core, p, me.r, y) * 2 + lax.rem(u, 2)]

    def plan(u, _):
        block = query_block(u)
        stream = jnp.int32(0)
        for n in range(1, STREAMS):
            stream = jnp.where(count[n] < count[stream], n, stream)

        def add(key_block, filled):
            at = table[0, key_block]
            p, r, y = split_ctx(lax.div(at, 2), me.core)
            slot = r * 8 + (y * 2 + pair_bit(p)) * 2 + lax.rem(at, 2)
            work[stream, filled] = (u * blocks + key_block) * 32 + slot
            return filled + jnp.where(lax.div(p, 2) == me.pair, 1, 0)

        count[stream] = lax.fori_loop(
            lax.div(table[1, block], half), block + 1, add, count[stream]
        )
        return 0

    lax.fori_loop(0, 16, plan, 0)
    steps = count[0]
    for n in range(1, STREAMS):
        steps = jnp.maximum(steps, count[n])
    for n in range(STREAMS):

        def fill(t, _):
            work[n, t] = (spare + n) * blocks * 32
            return 0

        lax.fori_loop(count[n], steps, fill, 0)

    def step(t, _):
        todo = []
        for n in range(STREAMS):
            code = work[n, t]
            slot = lax.rem(code, 32)
            key_block = lax.rem(lax.div(code, 32), blocks)
            u = lax.div(code, 32 * blocks)
            real = jnp.minimum(u, spare - 1)
            q_rows = pl.ds(pl.multiple_of(lax.rem(real, 2) * half, half), half)
            k_rows = pl.ds(pl.multiple_of(lax.rem(slot, 2) * half, half), half)
            r_k, m_k = lax.div(slot, 8), lax.rem(lax.div(slot, 2), 4)
            query = q[lax.div(real, 8), lax.rem(lax.div(real, 2), 4), q_rows, :]
            key, value = kv[r_k, m_k, 0, k_rows, :], kv[r_k, m_k, 1, k_rows, :]
            q_pos = query_block(real) * half + lax.broadcasted_iota(jnp.int32, (1, half), 1)
            todo.append((u, key_block, query, key, value, q_pos, lows[pl.ds(real, 1), :]))
        scores = [
            lax.dot_general(key, query, (((1,), (1,)), ((), ())), preferred_element_type=jnp.float32)
            for _, _, query, key, _, _, _ in todo
        ]
        for n, (u, key_block, _, _, value, q_pos, low) in enumerate(todo):
            k_pos = key_block * half + lax.broadcasted_iota(jnp.int32, (half, half), 0)
            masked = jnp.where((k_pos >= low) & (k_pos <= q_pos), scores[n], -1e30)
            old = top[u]
            new = jnp.maximum(old, jnp.max(masked, axis=0, keepdims=True))
            weights = jnp.exp2((masked - new) * (SCALE * LOG2E))
            factor = jnp.exp2((old - new) * (SCALE * LOG2E))
            top[u] = new
            total[u] = total[u] * factor + jnp.sum(weights, axis=0, keepdims=True)
            summed[u] = summed[u] * factor + lax.dot_general(
                value,
                weights.astype(jnp.bfloat16),
                (((0,), (0,)), ((), ())),
                preferred_element_type=jnp.float32,
            )
        return 0

    lax.fori_loop(0, steps, step, 0)

    def finish(u, _):
        at = (lax.div(u, 8), lax.rem(lax.div(u, 2), 4))
        rows = pl.ds(pl.multiple_of(lax.rem(u, 2) * half, half), half)
        some = total[u] > 0.0
        safe = jnp.where(some, total[u], 1.0)
        attended = (summed[u] * (1.0 / safe)).astype(out.dtype)
        for e in range(half // PART):
            chunk = lax.rem(u, 2) * (half // PART) + e
            out[at[0], at[1], chunk] = attended[:, e * PART : (e + 1) * PART]
        logs[at[0], at[1], :, rows] = jnp.where(some, top[u] * SCALE + jnp.log(safe), -1e30)
        return 0

    lax.fori_loop(0, 16, finish, 0)


def attend(table, lows, q, kv):
    rows = q.shape[2]
    half = rows // 2
    near = pl.BlockSpec(memory_space=pltpu.VMEM)
    return pl.pallas_call(
        attend_kernel,
        name="attend",
        out_shape=(
            jax.ShapeDtypeStruct((2, 4, rows // PART, HEAD, PART), q.dtype),
            jax.ShapeDtypeStruct((2, 4, 1, rows), jnp.float32),
        ),
        in_specs=[near] * 4,
        out_specs=(near, near),
        scratch_shapes=[
            pltpu.SMEM(table.shape, jnp.int32),
            pltpu.SMEM((STREAMS, 16 * BLOCKS + 1), jnp.int32),
            pltpu.SMEM((STREAMS,), jnp.int32),
            pltpu.VMEM((16 + STREAMS, 1, half), jnp.float32),
            pltpu.VMEM((16 + STREAMS, 1, half), jnp.float32),
            pltpu.VMEM((16 + STREAMS, HEAD, half), jnp.float32),
            pltpu.SemaphoreType.DMA((1,)),
        ],
        compiler_params=pltpu.CompilerParams(vmem_limit_bytes=VMEM_BYTES),
    )(table, lows, q, kv)


def project_kernel(
    o, logs, w_near, w_quarter, mixed, log_out,
    o_in, lo_in, merged, merged_logs, att, att_in, logs_in, w_far, total,
    own_sem, b_send, b_recv, lb_sem, a_send, a_recv, l_send, l_recv, x_send, x_recv, w_send, w_recv,
):
    me = Place()
    chunks = o.shape[2]
    left, right = lax.rem(me.r + 3, 4), lax.rem(me.r + 1, 4)
    wait_all = greet(
        [me.at_member(me.member(i)) for i in (1, 2, 3)]
        + [me.at_ring(left), me.at_ring(right), me.at_twin()]
        + [me.at_tp(me.mate), me.at_tp(me.across)]
    )
    own = [
        pltpu.make_async_copy(w_quarter.at[n], w_far.at[n, me.r], own_sem.at[n]) for n in (0, 1)
    ]
    for copy in own:
        copy.start()
    wait_all()
    sends = []

    def start(copy):
        copy.start()
        sends.append(copy)

    order = (3, 1, 2, 0)

    def to_twin(i, c):
        m = me.member(i)
        return remote(
            o.at[1 - me.pair, m, c], o_in.at[m, c], b_send.at[i, c], b_recv.at[i, c], me.at_twin()
        )

    def to_owner(i, c):
        return remote(
            merged.at[i - 1, c], att.at[c, :, head_columns(me.m)],
            a_send.at[i - 1, c], a_recv.at[i - 1, c], me.at_member(me.member(i)),
        )

    def log_to_owner(i):
        return remote(
            merged_logs.at[i], logs_in.at[me.m],
            l_send.at[i - 1], l_recv.at[i - 1], me.at_member(me.member(i)),
        )

    def pass_att(n, c):
        src = att_in.at[0, c] if n == 2 else att.at[c]
        to = me.across if n == 0 else me.mate
        return remote(src, att_in.at[n, c], x_send.at[n, c], x_recv.at[n, c], me.at_tp(to))

    def weights(n, rel, origin, to):
        slot = w_far.at[n, origin]
        return remote(slot, slot, w_send.at[n, rel], w_recv.at[n, rel], me.at_ring(to))

    def weights_arrived(n, rel):
        weights(n, rel, me.r, right).wait_recv()

    twin_logs = remote(logs.at[1 - me.pair], lo_in, lb_sem.at[0], lb_sem.at[1], me.at_twin())
    start(twin_logs)
    for c in range(chunks):
        for i in order:
            start(to_twin(i, c))
    twin_logs.wait_recv()
    shares = []
    for i in range(4):
        m = me.member(i)
        one, two = logs[me.pair, m], lo_in[m]
        most = jnp.maximum(one, two)
        e_one, e_two = jnp.exp(one - most), jnp.exp(two - most)
        both = e_one + e_two
        final = most + jnp.log(both)
        share = 1.0 / both
        shares.append((e_one * share, e_two * share))
        if i == 0:
            logs_in[me.m] = final
        else:
            merged_logs[i] = final
            start(log_to_owner(i))

    def merge(c):
        for i in order:
            m = me.member(i)
            lanes = slice(c * PART, (c + 1) * PART)
            to_twin(i, c).wait_recv()
            whole = (
                o[me.pair, m, c].astype(jnp.float32) * shares[i][0][:, lanes]
                + o_in[m, c].astype(jnp.float32) * shares[i][1][:, lanes]
            )
            turned = whole.T.astype(jnp.bfloat16)
            if i == 0:
                att[c, :, head_columns(me.m)] = turned
            else:
                merged[i - 1, c] = turned
                start(to_owner(i, c))

    def share_out(c):
        for i in (1, 2, 3):
            to_owner(i, c).wait_recv()
        start(pass_att(0, c))
        start(pass_att(1, c))
        total[c] = jnp.dot(att[c], w_near[0], preferred_element_type=jnp.float32)

    def far_weights(n):
        return w_far[n].reshape(w_near.shape[1:])

    def cross(c):
        pass_att(1, c).wait_recv()
        total[c] += jnp.dot(att_in[1, c], w_near[1], preferred_element_type=jnp.float32)
        pass_att(0, c).wait_recv()
        start(pass_att(2, c))

    def finish(c):
        both = total[c] + jnp.dot(
            att_in[0, c], far_weights(me.core), preferred_element_type=jnp.float32
        )
        pass_att(2, c).wait_recv()
        both += jnp.dot(
            att_in[2, c], far_weights(1 - me.core), preferred_element_type=jnp.float32
        )
        mixed[c * PART : (c + 1) * PART, :] = both.astype(mixed.dtype)

    for t in range(chunks + 3):
        if t < chunks:
            merge(t)
        if t == 0:
            for n in (0, 1):
                own[n].wait()
                start(weights(n, 0, me.r, right))
                start(weights(n, 1, me.r, left))
        if 0 <= t - 1 < chunks:
            share_out(t - 1)
        if t == 3:
            weights_arrived(0, 0)
            start(weights(0, 2, left, right))
            weights_arrived(1, 1)
            start(weights(1, 2, right, left))
        if 0 <= t - 2 < chunks:
            cross(t - 2)
        if t == chunks + 1:
            weights_arrived(0, 1)
            weights_arrived(1, 0)
            weights_arrived(0, 2)
            weights_arrived(1, 2)
            for c in range(chunks - 1):
                finish(c)
    finish(chunks - 1)
    for i in (1, 2, 3):
        log_to_owner(i).wait_recv()
    for h in range(4):
        log_out[h : h + 1, :] = logs_in[h]
    for copy in sends:
        copy.wait_send()


def project(o, logs, w_near, w_quarter):
    chunks, depth, columns = o.shape[2], w_near.shape[1], w_near.shape[2]
    rows = chunks * PART
    near = pl.BlockSpec(memory_space=pltpu.VMEM)
    dma = pltpu.SemaphoreType.DMA
    return pl.pallas_call(
        project_kernel,
        name="return_and_project",
        out_shape=(
            jax.ShapeDtypeStruct((rows, columns), jnp.bfloat16),
            jax.ShapeDtypeStruct((4, rows), jnp.float32),
        ),
        in_specs=[near] * 4,
        out_specs=(near, near),
        scratch_shapes=[
            pltpu.VMEM((4, chunks, HEAD, PART), jnp.bfloat16),
            pltpu.VMEM((4, 1, rows), jnp.float32),
            pltpu.VMEM((3, chunks, PART, HEAD), jnp.bfloat16),
            pltpu.VMEM((4, 1, rows), jnp.float32),
            pltpu.VMEM((chunks, PART, depth), jnp.bfloat16),
            pltpu.VMEM((3, chunks, PART, depth), jnp.bfloat16),
            pltpu.VMEM((4, 1, rows), jnp.float32),
            pltpu.VMEM((2, 4, depth // 4, columns), jnp.bfloat16),
            pltpu.VMEM((chunks, PART, columns), jnp.float32),
            dma((2,)), dma((4, chunks)), dma((4, chunks)), dma((2,)), dma((3, chunks)),
            dma((3, chunks)), dma((3,)), dma((3,)), dma((3, chunks)), dma((3, chunks)),
            dma((2, 3)), dma((2, 3)),
        ],
        compiler_params=pltpu.CompilerParams(
            collective_id=1, has_side_effects=True, vmem_limit_bytes=VMEM_BYTES
        ),
    )(o, logs, w_near, w_quarter)


def local(queries, keys, values, out_weight, doc_lengths, layout):
    held = (
        pltpu.with_memory_space_constraint(t, pltpu.HBM)
        for t in (queries, keys, values, out_weight, doc_lengths, layout)
    )
    qh, kv, w_near, w_quarter, table, lows = gather(*held)
    o, logs = attend(table, lows, qh, kv)
    return project(o, logs, w_near, w_quarter)


def solution(mesh):
    placed = (P("ctx", "tp"), P("ctx", "tp"), P("ctx", "tp"), P("tp", None), P(), P())
    return jax.shard_map(
        local,
        mesh=mesh,
        in_specs=placed,
        out_specs=(P("ctx", "tp"), P("tp", "ctx")),
        check_vma=False,
    )
```

```python
import math

import jax
import jax.numpy as jnp
from jax import lax
from jax.experimental import pallas as pl
from jax.experimental.pallas import tpu as pltpu
from jax.sharding import PartitionSpec as P

HEAD = 128
MESH = pl.DeviceIdType.MESH
SCALE = 1.0 / math.sqrt(HEAD)
LOG2E = math.log2(math.e)
STREAMS = 4
LEAST = -1e29
PART = 256
BLOCKS = 64
VMEM_BYTES = 40 * 1024 * 1024


def ctx_of(core, p, r, y):
    return p * (8 - 6 * core) + r * (2 + 6 * core) + y


def split_ctx(ctx, core):
    z, x, y = lax.div(ctx, 8), lax.rem(lax.div(ctx, 2), 4), lax.rem(ctx, 2)
    return z * (1 - core) + x * core, x * (1 - core) + z * core, y


def pair_bit(p):
    return lax.rem(lax.div(p + 1, 2), 2)


def member_place(pair, m):
    bit = lax.rem(m, 2)
    return bit + pair * (3 - 2 * bit), lax.div(m, 2)


class Place:
    def __init__(self):
        self.ctx, self.tp = lax.axis_index("ctx"), lax.axis_index("tp")
        self.core, self.high = lax.rem(self.tp, 2), lax.div(self.tp, 2)
        self.p, self.r, self.y = split_ctx(self.ctx, self.core)
        self.pair, self.bit = lax.div(self.p, 2), pair_bit(self.p)
        self.m = self.y * 2 + self.bit
        self.mate = self.high * 2 + 1 - self.core
        self.across = (1 - self.high) * 2 + self.core
        self.diagonal = (1 - self.high) * 2 + 1 - self.core

    def member(self, i):
        bit = 1 - self.bit if i % 2 else self.bit
        y = 1 - self.y if i // 2 else self.y
        return y * 2 + bit

    def at_member(self, m):
        p, y = member_place(self.pair, m)
        return (ctx_of(self.core, p, self.r, y), self.tp)

    def at_ring(self, r):
        return (ctx_of(self.core, self.p, r, self.y), self.tp)

    def at_tp(self, tp):
        return (self.ctx, tp)

    def at_twin(self):
        return (ctx_of(self.core, 3 - self.p, self.r, self.y), self.tp)


def head_columns(m):
    return pl.ds(pl.multiple_of(m * HEAD, HEAD), HEAD)


def remote(src, dst, send_sem, recv_sem, to):
    return pltpu.make_async_remote_copy(
        src_ref=src, dst_ref=dst, send_sem=send_sem, recv_sem=recv_sem,
        device_id=to, device_id_type=MESH,
    )


def greet(partners):
    barrier = pltpu.get_barrier_semaphore()
    for partner in partners:
        pl.semaphore_signal(barrier, inc=1, device_id=partner, device_id_type=MESH)
    return lambda: pl.semaphore_wait(barrier, len(partners))


def gather_kernel(
    q, k, v, w, far_lengths, far_layout, qh, kv, w_near, w_far, table, lows,
    lengths, layout, table_sem, own_sem, s_send, s_recv, g_send, g_recv, t_send, t_recv, w_send, w_recv,
):
    me = Place()
    left, right = lax.rem(me.r + 3, 4), lax.rem(me.r + 1, 4)
    wait_all = greet(
        [me.at_member(me.member(i)) for i in (1, 2, 3)]
        + [me.at_ring(left), me.at_ring(right), me.at_twin(), me.at_tp(me.mate)]
        + [me.at_tp(me.across), me.at_tp(me.diagonal)]
    )
    mine = head_columns(me.m)
    columns = w_near.shape[2]
    quarter = w_far.shape[1]

    def weight_columns(tp):
        return pl.ds(pl.multiple_of(tp * columns, columns), columns)

    own = [
        pltpu.make_async_copy(k.at[:, mine], kv.at[me.r, me.m, 0], own_sem.at[0]),
        pltpu.make_async_copy(v.at[:, mine], kv.at[me.r, me.m, 1], own_sem.at[1]),
        pltpu.make_async_copy(q.at[:, mine], qh.at[me.pair, me.m], own_sem.at[2]),
        pltpu.make_async_copy(w.at[:, weight_columns(me.tp)], w_near.at[0], own_sem.at[3]),
    ]
    own += [
        pltpu.make_async_copy(far_lengths, lengths, table_sem.at[0]),
        pltpu.make_async_copy(far_layout, layout, table_sem.at[1]),
    ]
    for copy in own:
        copy.start()
    wait_all()

    sends = []

    def start(copy):
        copy.start()
        sends.append(copy)

    def make_tables():
        own[4].wait()
        own[5].wait()
        half = lows.shape[1]
        lane = lax.broadcasted_iota(jnp.int32, (1, table.shape[1]), 1)
        row = lax.broadcasted_iota(jnp.int32, lows.shape, 0)
        q_pos = lax.broadcasted_iota(jnp.int32, lows.shape, 1)
        for u in range(16):
            p, y = member_place(u // 8, u // 2 % 4)
            block = layout[ctx_of(me.core, p, me.r, y) * 2 + u % 2]
            q_pos += jnp.where(row == u, block * half, 0)

        def place(b, state):
            where_is, held = state
            block = layout[b]
            return jnp.where(lane == block, b, where_is), jnp.where(lane == b, block, held)

        def walk(j, state):
            at, first, low = state
            first = jnp.where(lane * half >= at, at, first)
            low = jnp.where(q_pos >= at, at, low)
            return at + lengths[j], first, low

        none = jnp.zeros_like(lane)
        where_is, held = lax.fori_loop(0, layout.shape[0], place, (none, none))
        _, first, low = lax.fori_loop(
            0, lengths.shape[0], walk, (jnp.int32(0), none, jnp.zeros_like(q_pos))
        )
        table[0:1, :] = where_is
        table[1:2, :] = first
        table[2:3, :] = held
        lows[...] = low

    def spread(i, a):
        to = me.member(i)
        dst = qh.at[me.pair, me.m] if a == 2 else kv.at[me.r, me.m, a]
        return remote(
            (k, v, q)[a].at[:, head_columns(to)], dst,
            s_send.at[i - 1, a], s_recv.at[i - 1, a], me.at_member(to),
        )

    def ring(i, j, rel, origin, to):
        slot = kv.at[origin, me.member(i), j]
        return remote(slot, slot, g_send.at[i, j, rel], g_recv.at[i, j, rel], me.at_ring(to))

    def twin(i):
        slot = qh.at[me.pair, me.member(i)]
        return remote(slot, slot, t_send.at[i], t_recv.at[i], me.at_twin())

    def arrived(i, j, rel):
        ring(i, j, rel, me.r, right).wait_recv()

    def weights_across(n):
        to = (me.across, me.diagonal)[n]
        place = (me.r, me.p)[n]
        rows = pl.ds(pl.multiple_of(place * quarter, quarter), quarter)
        return remote(
            w.at[rows, weight_columns(to)], w_far.at[me.core],
            w_send.at[n], w_recv.at[n], me.at_tp(to),
        )

    weights_to_mate = remote(
        w.at[:, weight_columns(me.mate)], w_near.at[1], w_send.at[2], w_recv.at[2], me.at_tp(me.mate)
    )
    for a in (2, 0, 1):
        for i in (2, 3, 1):
            start(spread(i, a))

    def pass_query(i):
        if i == 0:
            own[2].wait()
        else:
            spread(i, 2).wait_recv()
        start(twin(i))

    def pass_weights():
        start(weights_across(0))
        start(weights_across(1))
        start(weights_to_mate)

    for i in range(5):
        if i < 4:
            for j in (0, 1):
                if i == 0:
                    own[j].wait()
                else:
                    spread(i, j).wait_recv()
                start(ring(i, j, 0, me.r, right))
                start(ring(i, j, 1, me.r, left))
        if i == 0:
            pass_query(0)
            make_tables()
            pass_query(1)
        if i == 1:
            pass_query(2)
            pass_query(3)
        if i == 2:
            pass_weights()
        if i >= 1:
            arrived(i - 1, 0, 0)
            start(ring(i - 1, 0, 2, left, right))
            arrived(i - 1, 1, 1)
            start(ring(i - 1, 1, 2, right, left))
    own[3].wait()
    for i in range(4):
        arrived(i, 0, 1)
        arrived(i, 1, 0)
        arrived(i, 0, 2)
        arrived(i, 1, 2)
        twin(i).wait_recv()
    weights_across(0).wait_recv()
    weights_across(1).wait_recv()
    weights_to_mate.wait_recv()
    for copy in sends:
        copy.wait_send()


def gather(q, k, v, w, lengths, layout):
    rows, depth, columns = q.shape[0], w.shape[0], w.shape[1] // 4
    anywhere, near = pl.BlockSpec(memory_space=pltpu.HBM), pl.BlockSpec(memory_space=pltpu.VMEM)
    dma = pltpu.SemaphoreType.DMA
    return pl.pallas_call(
        gather_kernel,
        name="spread_and_gather",
        out_shape=(
            jax.ShapeDtypeStruct((2, 4, rows, HEAD), q.dtype),
            jax.ShapeDtypeStruct((4, 4, 2, rows, HEAD), q.dtype),
            jax.ShapeDtypeStruct((2, depth, columns), w.dtype),
            jax.ShapeDtypeStruct((2, depth // 4, columns), w.dtype),
            jax.ShapeDtypeStruct((8, 128), jnp.int32),
            jax.ShapeDtypeStruct((16, rows // 2), jnp.int32),
        ),
        in_specs=[anywhere] * 6,
        out_specs=(near,) * 6,
        scratch_shapes=[
            pltpu.SMEM(lengths.shape, jnp.int32),
            pltpu.SMEM(layout.shape, jnp.int32),
            dma((2,)),
            dma((4,)), dma((3, 3)), dma((3, 3)), dma((4, 2, 3)), dma((4, 2, 3)), dma((4,)), dma((4,)),
            dma((3,)), dma((3,)),
        ],
        compiler_params=pltpu.CompilerParams(
            collective_id=0, has_side_effects=True, vmem_limit_bytes=VMEM_BYTES
        ),
    )(q, k, v, w, lengths, layout)


def attend_kernel(
    near_table, lows, q, kv, out, logs, table, work, count, top, total, summed, table_sem
):
    me = Place()
    blocks = BLOCKS
    half = q.shape[2] // 2
    spare = 16
    fetch = pltpu.make_async_copy(near_table, table, table_sem.at[0])
    fetch.start()
    top[...] = jnp.full(top.shape, LEAST, jnp.float32)
    total[...] = jnp.zeros(total.shape, jnp.float32)
    summed[...] = jnp.zeros(summed.shape, jnp.float32)
    for n in range(STREAMS):
        count[n] = 0
    fetch.wait()

    def query_block(u):
        p, y = member_place(lax.div(u, 8), lax.rem(lax.div(u, 2), 4))
        return table[2, ctx_of(me.core, p, me.r, y) * 2 + lax.rem(u, 2)]

    def plan(u, _):
        block = query_block(u)
        stream = jnp.int32(0)
        for n in range(1, STREAMS):
            stream = jnp.where(count[n] < count[stream], n, stream)

        def add(key_block, filled):
            at = table[0, key_block]
            p, r, y = split_ctx(lax.div(at, 2), me.core)
            slot = r * 8 + (y * 2 + pair_bit(p)) * 2 + lax.rem(at, 2)
            work[stream, filled] = (u * blocks + key_block) * 32 + slot
            return filled + jnp.where(lax.div(p, 2) == me.pair, 1, 0)

        count[stream] = lax.fori_loop(
            lax.div(table[1, block], half), block + 1, add, count[stream]
        )
        return 0

    lax.fori_loop(0, 16, plan, 0)
    steps = count[0]
    for n in range(1, STREAMS):
        steps = jnp.maximum(steps, count[n])
    for n in range(STREAMS):

        def fill(t, _):
            work[n, t] = (spare + n) * blocks * 32
            return 0

        lax.fori_loop(count[n], steps, fill, 0)

    def step(t, _):
        todo = []
        for n in range(STREAMS):
            code = work[n, t]
            slot = lax.rem(code, 32)
            key_block = lax.rem(lax.div(code, 32), blocks)
            u = lax.div(code, 32 * blocks)
            real = jnp.minimum(u, spare - 1)
            q_rows = pl.ds(pl.multiple_of(lax.rem(real, 2) * half, half), half)
            k_rows = pl.ds(pl.multiple_of(lax.rem(slot, 2) * half, half), half)
            r_k, m_k = lax.div(slot, 8), lax.rem(lax.div(slot, 2), 4)
            query = q[lax.div(real, 8), lax.rem(lax.div(real, 2), 4), q_rows, :]
            key, value = kv[r_k, m_k, 0, k_rows, :], kv[r_k, m_k, 1, k_rows, :]
            q_pos = query_block(real) * half + lax.broadcasted_iota(jnp.int32, (1, half), 1)
            todo.append((u, key_block, query, key, value, q_pos, lows[pl.ds(real, 1), :]))
        scores = [
            lax.dot_general(key, query, (((1,), (1,)), ((), ())), preferred_element_type=jnp.float32)
            for _, _, query, key, _, _, _ in todo
        ]
        for n, (u, key_block, _, _, value, q_pos, low) in enumerate(todo):
            k_pos = key_block * half + lax.broadcasted_iota(jnp.int32, (half, half), 0)
            masked = jnp.where((k_pos >= low) & (k_pos <= q_pos), scores[n], -1e30)
            old = top[u]
            new = jnp.maximum(old, jnp.max(masked, axis=0, keepdims=True))
            weights = jnp.exp2((masked - new) * (SCALE * LOG2E))
            factor = jnp.exp2((old - new) * (SCALE * LOG2E))
            top[u] = new
            total[u] = total[u] * factor + jnp.sum(weights, axis=0, keepdims=True)
            summed[u] = summed[u] * factor + lax.dot_general(
                value,
                weights.astype(jnp.bfloat16),
                (((0,), (0,)), ((), ())),
                preferred_element_type=jnp.float32,
            )
        return 0

    lax.fori_loop(0, steps, step, 0)

    def finish(u, _):
        at = (lax.div(u, 8), lax.rem(lax.div(u, 2), 4))
        rows = pl.ds(pl.multiple_of(lax.rem(u, 2) * half, half), half)
        some = total[u] > 0.0
        safe = jnp.where(some, total[u], 1.0)
        attended = (summed[u] * (1.0 / safe)).astype(out.dtype)
        for e in range(half // PART):
            chunk = lax.rem(u, 2) * (half // PART) + e
            out[at[0], at[1], chunk] = attended[:, e * PART : (e + 1) * PART]
        logs[at[0], at[1], :, rows] = jnp.where(some, top[u] * SCALE + jnp.log(safe), -1e30)
        return 0

    lax.fori_loop(0, 16, finish, 0)


def attend(table, lows, q, kv):
    rows = q.shape[2]
    half = rows // 2
    near = pl.BlockSpec(memory_space=pltpu.VMEM)
    return pl.pallas_call(
        attend_kernel,
        name="attend",
        out_shape=(
            jax.ShapeDtypeStruct((2, 4, rows // PART, HEAD, PART), q.dtype),
            jax.ShapeDtypeStruct((2, 4, 1, rows), jnp.float32),
        ),
        in_specs=[near] * 4,
        out_specs=(near, near),
        scratch_shapes=[
            pltpu.SMEM(table.shape, jnp.int32),
            pltpu.SMEM((STREAMS, 16 * BLOCKS + 1), jnp.int32),
            pltpu.SMEM((STREAMS,), jnp.int32),
            pltpu.VMEM((16 + STREAMS, 1, half), jnp.float32),
            pltpu.VMEM((16 + STREAMS, 1, half), jnp.float32),
            pltpu.VMEM((16 + STREAMS, HEAD, half), jnp.float32),
            pltpu.SemaphoreType.DMA((1,)),
        ],
        compiler_params=pltpu.CompilerParams(vmem_limit_bytes=VMEM_BYTES),
    )(table, lows, q, kv)


def project_kernel(
    o, logs, w_near, w_quarter, mixed, log_out,
    o_in, lo_in, merged, merged_logs, att, att_in, logs_in, w_far, total,
    own_sem, b_send, b_recv, lb_sem, a_send, a_recv, l_send, l_recv, x_send, x_recv, w_send, w_recv,
):
    me = Place()
    chunks = o.shape[2]
    left, right = lax.rem(me.r + 3, 4), lax.rem(me.r + 1, 4)
    wait_all = greet(
        [me.at_member(me.member(i)) for i in (1, 2, 3)]
        + [me.at_ring(left), me.at_ring(right), me.at_twin()]
        + [me.at_tp(me.mate), me.at_tp(me.across)]
    )
    own = [
        pltpu.make_async_copy(w_quarter.at[n], w_far.at[n, me.r], own_sem.at[n]) for n in (0, 1)
    ]
    for copy in own:
        copy.start()
    wait_all()
    sends = []

    def start(copy):
        copy.start()
        sends.append(copy)

    order = (3, 1, 2, 0)

    def to_twin(i, c):
        m = me.member(i)
        return remote(
            o.at[1 - me.pair, m, c], o_in.at[m, c], b_send.at[i, c], b_recv.at[i, c], me.at_twin()
        )

    def to_owner(i, c):
        return remote(
            merged.at[i - 1, c], att.at[c, :, head_columns(me.m)],
            a_send.at[i - 1, c], a_recv.at[i - 1, c], me.at_member(me.member(i)),
        )

    def log_to_owner(i):
        return remote(
            merged_logs.at[i], logs_in.at[me.m],
            l_send.at[i - 1], l_recv.at[i - 1], me.at_member(me.member(i)),
        )

    def pass_att(n, c):
        src = att_in.at[0, c] if n == 2 else att.at[c]
        to = me.across if n == 0 else me.mate
        return remote(src, att_in.at[n, c], x_send.at[n, c], x_recv.at[n, c], me.at_tp(to))

    def weights(n, rel, origin, to):
        slot = w_far.at[n, origin]
        return remote(slot, slot, w_send.at[n, rel], w_recv.at[n, rel], me.at_ring(to))

    def weights_arrived(n, rel):
        weights(n, rel, me.r, right).wait_recv()

    twin_logs = remote(logs.at[1 - me.pair], lo_in, lb_sem.at[0], lb_sem.at[1], me.at_twin())
    start(twin_logs)
    for c in range(chunks):
        for i in order:
            start(to_twin(i, c))
    twin_logs.wait_recv()
    shares = []
    for i in range(4):
        m = me.member(i)
        one, two = logs[me.pair, m], lo_in[m]
        most = jnp.maximum(one, two)
        e_one, e_two = jnp.exp(one - most), jnp.exp(two - most)
        both = e_one + e_two
        final = most + jnp.log(both)
        share = 1.0 / both
        shares.append((e_one * share, e_two * share))
        if i == 0:
            logs_in[me.m] = final
        else:
            merged_logs[i] = final
            start(log_to_owner(i))

    def merge(c):
        for i in order:
            m = me.member(i)
            lanes = slice(c * PART, (c + 1) * PART)
            to_twin(i, c).wait_recv()
            whole = (
                o[me.pair, m, c].astype(jnp.float32) * shares[i][0][:, lanes]
                + o_in[m, c].astype(jnp.float32) * shares[i][1][:, lanes]
            )
            turned = whole.T.astype(jnp.bfloat16)
            if i == 0:
                att[c, :, head_columns(me.m)] = turned
            else:
                merged[i - 1, c] = turned
                start(to_owner(i, c))

    def share_out(c):
        for i in (1, 2, 3):
            to_owner(i, c).wait_recv()
        start(pass_att(0, c))
        start(pass_att(1, c))
        total[c] = jnp.dot(att[c], w_near[0], preferred_element_type=jnp.float32)

    def far_weights(n):
        return w_far[n].reshape(w_near.shape[1:])

    def cross(c):
        pass_att(1, c).wait_recv()
        total[c] += jnp.dot(att_in[1, c], w_near[1], preferred_element_type=jnp.float32)
        pass_att(0, c).wait_recv()
        start(pass_att(2, c))

    def finish(c):
        both = total[c] + jnp.dot(
            att_in[0, c], far_weights(me.core), preferred_element_type=jnp.float32
        )
        pass_att(2, c).wait_recv()
        both += jnp.dot(
            att_in[2, c], far_weights(1 - me.core), preferred_element_type=jnp.float32
        )
        mixed[c * PART : (c + 1) * PART, :] = both.astype(mixed.dtype)

    for t in range(chunks + 3):
        if t < chunks:
            merge(t)
        if t == 1:
            for n in (0, 1):
                own[n].wait()
                start(weights(n, 0, me.r, right))
                start(weights(n, 1, me.r, left))
        if 0 <= t - 1 < chunks:
            share_out(t - 1)
        if t == 3:
            weights_arrived(0, 0)
            start(weights(0, 2, left, right))
            weights_arrived(1, 1)
            start(weights(1, 2, right, left))
        if 0 <= t - 2 < chunks:
            cross(t - 2)
        if t == chunks + 1:
            weights_arrived(0, 1)
            weights_arrived(1, 0)
            weights_arrived(0, 2)
            weights_arrived(1, 2)
            for c in range(chunks - 1):
                finish(c)
    finish(chunks - 1)
    for i in (1, 2, 3):
        log_to_owner(i).wait_recv()
    for h in range(4):
        log_out[h : h + 1, :] = logs_in[h]
    for copy in sends:
        copy.wait_send()


def project(o, logs, w_near, w_quarter):
    chunks, depth, columns = o.shape[2], w_near.shape[1], w_near.shape[2]
    rows = chunks * PART
    near = pl.BlockSpec(memory_space=pltpu.VMEM)
    dma = pltpu.SemaphoreType.DMA
    return pl.pallas_call(
        project_kernel,
        name="return_and_project",
        out_shape=(
            jax.ShapeDtypeStruct((rows, columns), jnp.bfloat16),
            jax.ShapeDtypeStruct((4, rows), jnp.float32),
        ),
        in_specs=[near] * 4,
        out_specs=(near, near),
        scratch_shapes=[
            pltpu.VMEM((4, chunks, HEAD, PART), jnp.bfloat16),
            pltpu.VMEM((4, 1, rows), jnp.float32),
            pltpu.VMEM((3, chunks, PART, HEAD), jnp.bfloat16),
            pltpu.VMEM((4, 1, rows), jnp.float32),
            pltpu.VMEM((chunks, PART, depth), jnp.bfloat16),
            pltpu.VMEM((3, chunks, PART, depth), jnp.bfloat16),
            pltpu.VMEM((4, 1, rows), jnp.float32),
            pltpu.VMEM((2, 4, depth // 4, columns), jnp.bfloat16),
            pltpu.VMEM((chunks, PART, columns), jnp.float32),
            dma((2,)), dma((4, chunks)), dma((4, chunks)), dma((2,)), dma((3, chunks)),
            dma((3, chunks)), dma((3,)), dma((3,)), dma((3, chunks)), dma((3, chunks)),
            dma((2, 3)), dma((2, 3)),
        ],
        compiler_params=pltpu.CompilerParams(
            collective_id=1, has_side_effects=True, vmem_limit_bytes=VMEM_BYTES
        ),
    )(o, logs, w_near, w_quarter)


def local(queries, keys, values, out_weight, doc_lengths, layout):
    held = (
        pltpu.with_memory_space_constraint(t, pltpu.HBM)
        for t in (queries, keys, values, out_weight, doc_lengths, layout)
    )
    qh, kv, w_near, w_quarter, table, lows = gather(*held)
    o, logs = attend(table, lows, qh, kv)
    return project(o, logs, w_near, w_quarter)


def solution(mesh):
    placed = (P("ctx", "tp"), P("ctx", "tp"), P("ctx", "tp"), P("tp", None), P(), P())
    return jax.shard_map(
        local,
        mesh=mesh,
        in_specs=placed,
        out_specs=(P("ctx", "tp"), P("tp", "ctx")),
        check_vma=False,
    )
```

```python
import math

import jax
import jax.numpy as jnp
from jax import lax
from jax.experimental import pallas as pl
from jax.experimental.pallas import tpu as pltpu
from jax.sharding import PartitionSpec as P

HEAD = 128
MESH = pl.DeviceIdType.MESH
SCALE = 1.0 / math.sqrt(HEAD)
LOG2E = math.log2(math.e)
STREAMS = 4
LEAST = -1e29
PART = 128
BLOCKS = 64
VMEM_BYTES = 40 * 1024 * 1024


def ctx_of(core, p, r, y):
    return p * (8 - 6 * core) + r * (2 + 6 * core) + y


def split_ctx(ctx, core):
    z, x, y = lax.div(ctx, 8), lax.rem(lax.div(ctx, 2), 4), lax.rem(ctx, 2)
    return z * (1 - core) + x * core, x * (1 - core) + z * core, y


def pair_bit(p):
    return lax.rem(lax.div(p + 1, 2), 2)


def member_place(pair, m):
    bit = lax.rem(m, 2)
    return bit + pair * (3 - 2 * bit), lax.div(m, 2)


class Place:
    def __init__(self):
        self.ctx, self.tp = lax.axis_index("ctx"), lax.axis_index("tp")
        self.core, self.high = lax.rem(self.tp, 2), lax.div(self.tp, 2)
        self.p, self.r, self.y = split_ctx(self.ctx, self.core)
        self.pair, self.bit = lax.div(self.p, 2), pair_bit(self.p)
        self.m = self.y * 2 + self.bit
        self.mate = self.high * 2 + 1 - self.core
        self.across = (1 - self.high) * 2 + self.core
        self.diagonal = (1 - self.high) * 2 + 1 - self.core

    def member(self, i):
        bit = 1 - self.bit if i % 2 else self.bit
        y = 1 - self.y if i // 2 else self.y
        return y * 2 + bit

    def at_member(self, m):
        p, y = member_place(self.pair, m)
        return (ctx_of(self.core, p, self.r, y), self.tp)

    def at_ring(self, r):
        return (ctx_of(self.core, self.p, r, self.y), self.tp)

    def at_tp(self, tp):
        return (self.ctx, tp)

    def at_twin(self):
        return (ctx_of(self.core, 3 - self.p, self.r, self.y), self.tp)


def head_columns(m):
    return pl.ds(pl.multiple_of(m * HEAD, HEAD), HEAD)


def remote(src, dst, send_sem, recv_sem, to):
    return pltpu.make_async_remote_copy(
        src_ref=src, dst_ref=dst, send_sem=send_sem, recv_sem=recv_sem,
        device_id=to, device_id_type=MESH,
    )


def greet(partners):
    barrier = pltpu.get_barrier_semaphore()
    for partner in partners:
        pl.semaphore_signal(barrier, inc=1, device_id=partner, device_id_type=MESH)
    return lambda: pl.semaphore_wait(barrier, len(partners))


def gather_kernel(
    q, k, v, w, far_lengths, far_layout, qh, kv, w_near, w_far, table, lows,
    lengths, layout, table_sem, own_sem, s_send, s_recv, g_send, g_recv, t_send, t_recv, w_send, w_recv,
):
    me = Place()
    left, right = lax.rem(me.r + 3, 4), lax.rem(me.r + 1, 4)
    wait_all = greet(
        [me.at_member(me.member(i)) for i in (1, 2, 3)]
        + [me.at_ring(left), me.at_ring(right), me.at_twin(), me.at_tp(me.mate)]
        + [me.at_tp(me.across), me.at_tp(me.diagonal)]
    )
    mine = head_columns(me.m)
    columns = w_near.shape[2]
    quarter = w_far.shape[1]

    def weight_columns(tp):
        return pl.ds(pl.multiple_of(tp * columns, columns), columns)

    own = [
        pltpu.make_async_copy(k.at[:, mine], kv.at[me.r, me.m, 0], own_sem.at[0]),
        pltpu.make_async_copy(v.at[:, mine], kv.at[me.r, me.m, 1], own_sem.at[1]),
        pltpu.make_async_copy(q.at[:, mine], qh.at[me.pair, me.m], own_sem.at[2]),
        pltpu.make_async_copy(w.at[:, weight_columns(me.tp)], w_near.at[0], own_sem.at[3]),
    ]
    own += [
        pltpu.make_async_copy(far_lengths, lengths, table_sem.at[0]),
        pltpu.make_async_copy(far_layout, layout, table_sem.at[1]),
    ]
    for copy in own:
        copy.start()
    wait_all()

    sends = []

    def start(copy):
        copy.start()
        sends.append(copy)

    def make_tables():
        own[4].wait()
        own[5].wait()
        half = lows.shape[1]
        lane = lax.broadcasted_iota(jnp.int32, (1, table.shape[1]), 1)
        row = lax.broadcasted_iota(jnp.int32, lows.shape, 0)
        q_pos = lax.broadcasted_iota(jnp.int32, lows.shape, 1)
        for u in range(16):
            p, y = member_place(u // 8, u // 2 % 4)
            block = layout[ctx_of(me.core, p, me.r, y) * 2 + u % 2]
            q_pos += jnp.where(row == u, block * half, 0)

        def place(b, state):
            where_is, held = state
            block = layout[b]
            return jnp.where(lane == block, b, where_is), jnp.where(lane == b, block, held)

        def walk(j, state):
            at, first, low = state
            first = jnp.where(lane * half >= at, at, first)
            low = jnp.where(q_pos >= at, at, low)
            return at + lengths[j], first, low

        none = jnp.zeros_like(lane)
        where_is, held = lax.fori_loop(0, layout.shape[0], place, (none, none))
        _, first, low = lax.fori_loop(
            0, lengths.shape[0], walk, (jnp.int32(0), none, jnp.zeros_like(q_pos))
        )
        table[0:1, :] = where_is
        table[1:2, :] = first // half
        table[2:3, :] = held
        device = where_is // 2
        z, x, y = device // 8, device // 2 % 4, device % 2
        p, r = z * (1 - me.core) + x * me.core, x * (1 - me.core) + z * me.core
        table[3:4, :] = r * 8 + (y * 2 + (p + 1) // 2 % 2) * 2 + where_is % 2
        table[4:5, :] = jnp.where(p // 2 == me.pair, 1, 0)
        lows[...] = low

    def spread(i, a):
        to = me.member(i)
        dst = qh.at[me.pair, me.m] if a == 2 else kv.at[me.r, me.m, a]
        return remote(
            (k, v, q)[a].at[:, head_columns(to)], dst,
            s_send.at[i - 1, a], s_recv.at[i - 1, a], me.at_member(to),
        )

    def ring(i, j, rel, origin, to):
        slot = kv.at[origin, me.member(i), j]
        return remote(slot, slot, g_send.at[i, j, rel], g_recv.at[i, j, rel], me.at_ring(to))

    def twin(i):
        slot = qh.at[me.pair, me.member(i)]
        return remote(slot, slot, t_send.at[i], t_recv.at[i], me.at_twin())

    def arrived(i, j, rel):
        ring(i, j, rel, me.r, right).wait_recv()

    def weights_across(n):
        to = (me.across, me.diagonal)[n]
        place = (me.r, me.p)[n]
        rows = pl.ds(pl.multiple_of(place * quarter, quarter), quarter)
        return remote(
            w.at[rows, weight_columns(to)], w_far.at[me.core],
            w_send.at[n], w_recv.at[n], me.at_tp(to),
        )

    weights_to_mate = remote(
        w.at[:, weight_columns(me.mate)], w_near.at[1], w_send.at[2], w_recv.at[2], me.at_tp(me.mate)
    )
    for a in (2, 0, 1):
        for i in (2, 3, 1):
            start(spread(i, a))

    def pass_query(i):
        if i == 0:
            own[2].wait()
        else:
            spread(i, 2).wait_recv()
        start(twin(i))

    def pass_weights():
        start(weights_across(0))
        start(weights_across(1))
        start(weights_to_mate)

    for i in range(5):
        if i < 4:
            for j in (0, 1):
                if i == 0:
                    own[j].wait()
                else:
                    spread(i, j).wait_recv()
                start(ring(i, j, 0, me.r, right))
                start(ring(i, j, 1, me.r, left))
        if i == 0:
            pass_query(0)
            make_tables()
            pass_query(1)
        if i == 1:
            pass_query(2)
            pass_query(3)
        if i == 2:
            pass_weights()
        if i >= 1:
            arrived(i - 1, 0, 0)
            start(ring(i - 1, 0, 2, left, right))
            arrived(i - 1, 1, 1)
            start(ring(i - 1, 1, 2, right, left))
    own[3].wait()
    for i in range(4):
        arrived(i, 0, 1)
        arrived(i, 1, 0)
        arrived(i, 0, 2)
        arrived(i, 1, 2)
        twin(i).wait_recv()
    weights_across(0).wait_recv()
    weights_across(1).wait_recv()
    weights_to_mate.wait_recv()
    for copy in sends:
        copy.wait_send()


def gather(q, k, v, w, lengths, layout):
    rows, depth, columns = q.shape[0], w.shape[0], w.shape[1] // 4
    anywhere, near = pl.BlockSpec(memory_space=pltpu.HBM), pl.BlockSpec(memory_space=pltpu.VMEM)
    dma = pltpu.SemaphoreType.DMA
    return pl.pallas_call(
        gather_kernel,
        name="spread_and_gather",
        out_shape=(
            jax.ShapeDtypeStruct((2, 4, rows, HEAD), q.dtype),
            jax.ShapeDtypeStruct((4, 4, 2, rows, HEAD), q.dtype),
            jax.ShapeDtypeStruct((2, depth, columns), w.dtype),
            jax.ShapeDtypeStruct((2, depth // 4, columns), w.dtype),
            jax.ShapeDtypeStruct((8, 128), jnp.int32),
            jax.ShapeDtypeStruct((16, rows // 2), jnp.int32),
        ),
        in_specs=[anywhere] * 6,
        out_specs=(near,) * 6,
        scratch_shapes=[
            pltpu.SMEM(lengths.shape, jnp.int32),
            pltpu.SMEM(layout.shape, jnp.int32),
            dma((2,)),
            dma((4,)), dma((3, 3)), dma((3, 3)), dma((4, 2, 3)), dma((4, 2, 3)), dma((4,)), dma((4,)),
            dma((3,)), dma((3,)),
        ],
        compiler_params=pltpu.CompilerParams(
            collective_id=0, has_side_effects=True, vmem_limit_bytes=VMEM_BYTES
        ),
    )(q, k, v, w, lengths, layout)


def attend_kernel(
    near_table, lows, q, kv, out, logs, table, work, count, top, total, summed, table_sem
):
    me = Place()
    blocks = BLOCKS
    half = q.shape[2] // 2
    spare = 16
    fetch = pltpu.make_async_copy(near_table, table, table_sem.at[0])
    fetch.start()
    top[...] = jnp.full(top.shape, LEAST, jnp.float32)
    total[...] = jnp.zeros(total.shape, jnp.float32)
    summed[...] = jnp.zeros(summed.shape, jnp.float32)
    for n in range(STREAMS):
        count[n] = 0
    fetch.wait()

    def query_block(u):
        p, y = member_place(lax.div(u, 8), lax.rem(lax.div(u, 2), 4))
        return table[2, ctx_of(me.core, p, me.r, y) * 2 + lax.rem(u, 2)]

    def plan(u, _):
        block = query_block(u)
        stream = jnp.int32(0)
        for n in range(1, STREAMS):
            stream = jnp.where(count[n] < count[stream], n, stream)

        def add(key_block, filled):
            work[stream, filled] = (u * blocks + key_block) * 32 + table[3, key_block]
            return filled + table[4, key_block]

        count[stream] = lax.fori_loop(
            table[1, block], block + 1, add, count[stream]
        )
        return 0

    lax.fori_loop(0, 16, plan, 0)
    steps = count[0]
    for n in range(1, STREAMS):
        steps = jnp.maximum(steps, count[n])
    for n in range(STREAMS):

        def fill(t, _):
            work[n, t] = (spare + n) * blocks * 32
            return 0

        lax.fori_loop(count[n], steps, fill, 0)

    def step(t, _):
        todo = []
        for n in range(STREAMS):
            code = work[n, t]
            slot = lax.rem(code, 32)
            key_block = lax.rem(lax.div(code, 32), blocks)
            u = lax.div(code, 32 * blocks)
            real = jnp.minimum(u, spare - 1)
            q_rows = pl.ds(pl.multiple_of(lax.rem(real, 2) * half, half), half)
            k_rows = pl.ds(pl.multiple_of(lax.rem(slot, 2) * half, half), half)
            r_k, m_k = lax.div(slot, 8), lax.rem(lax.div(slot, 2), 4)
            query = q[lax.div(real, 8), lax.rem(lax.div(real, 2), 4), q_rows, :]
            key, value = kv[r_k, m_k, 0, k_rows, :], kv[r_k, m_k, 1, k_rows, :]
            q_pos = query_block(real) * half + lax.broadcasted_iota(jnp.int32, (1, half), 1)
            todo.append((u, key_block, query, key, value, q_pos, lows[pl.ds(real, 1), :]))
        scores = [
            lax.dot_general(key, query, (((1,), (1,)), ((), ())), preferred_element_type=jnp.float32)
            for _, _, query, key, _, _, _ in todo
        ]
        for n, (u, key_block, _, _, value, q_pos, low) in enumerate(todo):
            k_pos = key_block * half + lax.broadcasted_iota(jnp.int32, (half, half), 0)
            masked = jnp.where((k_pos >= low) & (k_pos <= q_pos), scores[n], -1e30)
            old = top[u]
            new = jnp.maximum(old, jnp.max(masked, axis=0, keepdims=True))
            weights = jnp.exp2((masked - new) * (SCALE * LOG2E))
            factor = jnp.exp2((old - new) * (SCALE * LOG2E))
            top[u] = new
            total[u] = total[u] * factor + jnp.sum(weights, axis=0, keepdims=True)
            summed[u] = summed[u] * factor + lax.dot_general(
                value,
                weights.astype(jnp.bfloat16),
                (((0,), (0,)), ((), ())),
                preferred_element_type=jnp.float32,
            )
        return 0

    lax.fori_loop(0, steps, step, 0)

    def finish(u, _):
        at = (lax.div(u, 8), lax.rem(lax.div(u, 2), 4))
        rows = pl.ds(pl.multiple_of(lax.rem(u, 2) * half, half), half)
        some = total[u] > 0.0
        safe = jnp.where(some, total[u], 1.0)
        attended = (summed[u] * (1.0 / safe)).astype(out.dtype)
        for e in range(half // PART):
            chunk = lax.rem(u, 2) * (half // PART) + e
            out[at[0], at[1], chunk] = attended[:, e * PART : (e + 1) * PART]
        logs[at[0], at[1], :, rows] = jnp.where(some, top[u] * SCALE + jnp.log(safe), -1e30)
        return 0

    lax.fori_loop(0, 16, finish, 0)


def attend(table, lows, q, kv):
    rows = q.shape[2]
    half = rows // 2
    near = pl.BlockSpec(memory_space=pltpu.VMEM)
    return pl.pallas_call(
        attend_kernel,
        name="attend",
        out_shape=(
            jax.ShapeDtypeStruct((2, 4, rows // PART, HEAD, PART), q.dtype),
            jax.ShapeDtypeStruct((2, 4, 1, rows), jnp.float32),
        ),
        in_specs=[near] * 4,
        out_specs=(near, near),
        scratch_shapes=[
            pltpu.SMEM(table.shape, jnp.int32),
            pltpu.SMEM((STREAMS, 16 * BLOCKS + 1), jnp.int32),
            pltpu.SMEM((STREAMS,), jnp.int32),
            pltpu.VMEM((16 + STREAMS, 1, half), jnp.float32),
            pltpu.VMEM((16 + STREAMS, 1, half), jnp.float32),
            pltpu.VMEM((16 + STREAMS, HEAD, half), jnp.float32),
            pltpu.SemaphoreType.DMA((1,)),
        ],
        compiler_params=pltpu.CompilerParams(vmem_limit_bytes=VMEM_BYTES),
    )(table, lows, q, kv)


def project_kernel(
    o, logs, w_near, w_quarter, mixed, log_out,
    o_in, lo_in, merged, merged_logs, att, att_in, logs_in, w_far, total,
    own_sem, b_send, b_recv, lb_sem, a_send, a_recv, l_send, l_recv, x_send, x_recv, w_send, w_recv,
):
    me = Place()
    chunks = o.shape[2]
    left, right = lax.rem(me.r + 3, 4), lax.rem(me.r + 1, 4)
    wait_all = greet(
        [me.at_member(me.member(i)) for i in (1, 2, 3)]
        + [me.at_ring(left), me.at_ring(right), me.at_twin()]
        + [me.at_tp(me.mate), me.at_tp(me.across)]
    )
    own = [
        pltpu.make_async_copy(w_quarter.at[n], w_far.at[n, me.r], own_sem.at[n]) for n in (0, 1)
    ]
    for copy in own:
        copy.start()
    wait_all()
    sends = []

    def start(copy):
        copy.start()
        sends.append(copy)

    order = (3, 1, 2, 0)

    def to_twin(i, c):
        m = me.member(i)
        return remote(
            o.at[1 - me.pair, m, c], o_in.at[m, c], b_send.at[i, c], b_recv.at[i, c], me.at_twin()
        )

    def to_owner(i, c):
        return remote(
            merged.at[i - 1, c], att.at[c, :, head_columns(me.m)],
            a_send.at[i - 1, c], a_recv.at[i - 1, c], me.at_member(me.member(i)),
        )

    def log_to_owner(i):
        return remote(
            merged_logs.at[i], logs_in.at[me.m],
            l_send.at[i - 1], l_recv.at[i - 1], me.at_member(me.member(i)),
        )

    def pass_att(n, c):
        src = att_in.at[0, c] if n == 2 else att.at[c]
        to = me.across if n == 0 else me.mate
        return remote(src, att_in.at[n, c], x_send.at[n, c], x_recv.at[n, c], me.at_tp(to))

    def weights(n, rel, origin, to):
        slot = w_far.at[n, origin]
        return remote(slot, slot, w_send.at[n, rel], w_recv.at[n, rel], me.at_ring(to))

    def weights_arrived(n, rel):
        weights(n, rel, me.r, right).wait_recv()

    twin_logs = remote(logs.at[1 - me.pair], lo_in, lb_sem.at[0], lb_sem.at[1], me.at_twin())
    start(twin_logs)
    for c in range(chunks):
        for i in order:
            start(to_twin(i, c))
    twin_logs.wait_recv()
    shares = []
    for i in range(4):
        m = me.member(i)
        one, two = logs[me.pair, m], lo_in[m]
        most = jnp.maximum(one, two)
        e_one, e_two = jnp.exp(one - most), jnp.exp(two - most)
        both = e_one + e_two
        final = most + jnp.log(both)
        share = 1.0 / both
        shares.append((e_one * share, e_two * share))
        if i == 0:
            logs_in[me.m] = final
        else:
            merged_logs[i] = final
            start(log_to_owner(i))

    def merge(c):
        for i in order:
            m = me.member(i)
            lanes = slice(c * PART, (c + 1) * PART)
            to_twin(i, c).wait_recv()
            whole = (
                o[me.pair, m, c].astype(jnp.float32) * shares[i][0][:, lanes]
                + o_in[m, c].astype(jnp.float32) * shares[i][1][:, lanes]
            )
            turned = whole.T.astype(jnp.bfloat16)
            if i == 0:
                att[c, :, head_columns(me.m)] = turned
            else:
                merged[i - 1, c] = turned
                start(to_owner(i, c))

    def share_out(c):
        for i in (1, 2, 3):
            to_owner(i, c).wait_recv()
        start(pass_att(0, c))
        start(pass_att(1, c))
        total[c] = jnp.dot(att[c], w_near[0], preferred_element_type=jnp.float32)

    def far_weights(n):
        return w_far[n].reshape(w_near.shape[1:])

    def cross(c):
        pass_att(1, c).wait_recv()
        total[c] += jnp.dot(att_in[1, c], w_near[1], preferred_element_type=jnp.float32)
        pass_att(0, c).wait_recv()
        start(pass_att(2, c))

    def finish(c):
        both = total[c] + jnp.dot(
            att_in[0, c], far_weights(me.core), preferred_element_type=jnp.float32
        )
        pass_att(2, c).wait_recv()
        both += jnp.dot(
            att_in[2, c], far_weights(1 - me.core), preferred_element_type=jnp.float32
        )
        mixed[c * PART : (c + 1) * PART, :] = both.astype(mixed.dtype)

    for t in range(chunks + 3):
        if t < chunks:
            merge(t)
        if t == 0:
            for n in (0, 1):
                own[n].wait()
                start(weights(n, 0, me.r, right))
                start(weights(n, 1, me.r, left))
        if 0 <= t - 1 < chunks:
            share_out(t - 1)
        if t == 3:
            weights_arrived(0, 0)
            start(weights(0, 2, left, right))
            weights_arrived(1, 1)
            start(weights(1, 2, right, left))
        if 0 <= t - 2 < chunks:
            cross(t - 2)
        if t == chunks + 1:
            weights_arrived(0, 1)
            weights_arrived(1, 0)
            weights_arrived(0, 2)
            weights_arrived(1, 2)
            for c in range(chunks - 1):
                finish(c)
    finish(chunks - 1)
    for i in (1, 2, 3):
        log_to_owner(i).wait_recv()
    for h in range(4):
        log_out[h : h + 1, :] = logs_in[h]
    for copy in sends:
        copy.wait_send()


def project(o, logs, w_near, w_quarter):
    chunks, depth, columns = o.shape[2], w_near.shape[1], w_near.shape[2]
    rows = chunks * PART
    near = pl.BlockSpec(memory_space=pltpu.VMEM)
    dma = pltpu.SemaphoreType.DMA
    return pl.pallas_call(
        project_kernel,
        name="return_and_project",
        out_shape=(
            jax.ShapeDtypeStruct((rows, columns), jnp.bfloat16),
            jax.ShapeDtypeStruct((4, rows), jnp.float32),
        ),
        in_specs=[near] * 4,
        out_specs=(near, near),
        scratch_shapes=[
            pltpu.VMEM((4, chunks, HEAD, PART), jnp.bfloat16),
            pltpu.VMEM((4, 1, rows), jnp.float32),
            pltpu.VMEM((3, chunks, PART, HEAD), jnp.bfloat16),
            pltpu.VMEM((4, 1, rows), jnp.float32),
            pltpu.VMEM((chunks, PART, depth), jnp.bfloat16),
            pltpu.VMEM((3, chunks, PART, depth), jnp.bfloat16),
            pltpu.VMEM((4, 1, rows), jnp.float32),
            pltpu.VMEM((2, 4, depth // 4, columns), jnp.bfloat16),
            pltpu.VMEM((chunks, PART, columns), jnp.float32),
            dma((2,)), dma((4, chunks)), dma((4, chunks)), dma((2,)), dma((3, chunks)),
            dma((3, chunks)), dma((3,)), dma((3,)), dma((3, chunks)), dma((3, chunks)),
            dma((2, 3)), dma((2, 3)),
        ],
        compiler_params=pltpu.CompilerParams(
            collective_id=1, has_side_effects=True, vmem_limit_bytes=VMEM_BYTES
        ),
    )(o, logs, w_near, w_quarter)


def local(queries, keys, values, out_weight, doc_lengths, layout):
    held = (
        pltpu.with_memory_space_constraint(t, pltpu.HBM)
        for t in (queries, keys, values, out_weight, doc_lengths, layout)
    )
    qh, kv, w_near, w_quarter, table, lows = gather(*held)
    o, logs = attend(table, lows, qh, kv)
    return project(o, logs, w_near, w_quarter)


def solution(mesh):
    placed = (P("ctx", "tp"), P("ctx", "tp"), P("ctx", "tp"), P("tp", None), P(), P())
    return jax.shard_map(
        local,
        mesh=mesh,
        in_specs=placed,
        out_specs=(P("ctx", "tp"), P("tp", "ctx")),
        check_vma=False,
    )
```

```python
import math

import jax
import jax.numpy as jnp
from jax import lax
from jax.experimental import pallas as pl
from jax.experimental.pallas import tpu as pltpu
from jax.sharding import PartitionSpec as P

HEAD = 128
MESH = pl.DeviceIdType.MESH
SCALE = 1.0 / math.sqrt(HEAD)
LOG2E = math.log2(math.e)
STREAMS = 4
LEAST = -1e29
PART = 128
BLOCKS = 64
VMEM_BYTES = 40 * 1024 * 1024


def ctx_of(core, p, r, y):
    return p * (8 - 6 * core) + r * (2 + 6 * core) + y


def split_ctx(ctx, core):
    z, x, y = lax.div(ctx, 8), lax.rem(lax.div(ctx, 2), 4), lax.rem(ctx, 2)
    return z * (1 - core) + x * core, x * (1 - core) + z * core, y


def pair_bit(p):
    return lax.rem(lax.div(p + 1, 2), 2)


def member_place(pair, m):
    bit = lax.rem(m, 2)
    return bit + pair * (3 - 2 * bit), lax.div(m, 2)


class Place:
    def __init__(self):
        self.ctx, self.tp = lax.axis_index("ctx"), lax.axis_index("tp")
        self.core, self.high = lax.rem(self.tp, 2), lax.div(self.tp, 2)
        self.p, self.r, self.y = split_ctx(self.ctx, self.core)
        self.pair, self.bit = lax.div(self.p, 2), pair_bit(self.p)
        self.m = self.y * 2 + self.bit
        self.mate = self.high * 2 + 1 - self.core
        self.across = (1 - self.high) * 2 + self.core
        self.diagonal = (1 - self.high) * 2 + 1 - self.core

    def member(self, i):
        bit = 1 - self.bit if i % 2 else self.bit
        y = 1 - self.y if i // 2 else self.y
        return y * 2 + bit

    def at_member(self, m):
        p, y = member_place(self.pair, m)
        return (ctx_of(self.core, p, self.r, y), self.tp)

    def at_ring(self, r):
        return (ctx_of(self.core, self.p, r, self.y), self.tp)

    def at_tp(self, tp):
        return (self.ctx, tp)

    def at_twin(self):
        return (ctx_of(self.core, 3 - self.p, self.r, self.y), self.tp)


def head_columns(m):
    return pl.ds(pl.multiple_of(m * HEAD, HEAD), HEAD)


def remote(src, dst, send_sem, recv_sem, to):
    return pltpu.make_async_remote_copy(
        src_ref=src, dst_ref=dst, send_sem=send_sem, recv_sem=recv_sem,
        device_id=to, device_id_type=MESH,
    )


def greet(partners):
    barrier = pltpu.get_barrier_semaphore()
    for partner in partners:
        pl.semaphore_signal(barrier, inc=1, device_id=partner, device_id_type=MESH)
    return lambda: pl.semaphore_wait(barrier, len(partners))


def gather_kernel(
    q, k, v, w, far_lengths, far_layout, qh, kv, w_near, w_far, table, lows,
    lengths, layout, table_sem, own_sem, s_send, s_recv, g_send, g_recv, t_send, t_recv, w_send, w_recv,
):
    me = Place()
    left, right = lax.rem(me.r + 3, 4), lax.rem(me.r + 1, 4)
    wait_all = greet(
        [me.at_member(me.member(i)) for i in (1, 2, 3)]
        + [me.at_ring(left), me.at_ring(right), me.at_twin(), me.at_tp(me.mate)]
        + [me.at_tp(me.across), me.at_tp(me.diagonal)]
    )
    mine = head_columns(me.m)
    columns = w_near.shape[2]
    quarter = w_far.shape[1]

    def weight_columns(tp):
        return pl.ds(pl.multiple_of(tp * columns, columns), columns)

    own = [
        pltpu.make_async_copy(k.at[:, mine], kv.at[me.r, me.m, 0], own_sem.at[0]),
        pltpu.make_async_copy(v.at[:, mine], kv.at[me.r, me.m, 1], own_sem.at[1]),
        pltpu.make_async_copy(q.at[:, mine], qh.at[me.pair, me.m], own_sem.at[2]),
        pltpu.make_async_copy(w.at[:, weight_columns(me.tp)], w_near.at[0], own_sem.at[3]),
    ]
    own += [
        pltpu.make_async_copy(far_lengths, lengths, table_sem.at[0]),
        pltpu.make_async_copy(far_layout, layout, table_sem.at[1]),
    ]
    for copy in own:
        copy.start()
    wait_all()

    sends = []

    def start(copy):
        copy.start()
        sends.append(copy)

    def make_tables():
        own[4].wait()
        own[5].wait()
        half = lows.shape[1]
        lane = lax.broadcasted_iota(jnp.int32, (1, table.shape[1]), 1)
        row = lax.broadcasted_iota(jnp.int32, lows.shape, 0)
        q_pos = lax.broadcasted_iota(jnp.int32, lows.shape, 1)
        wanted = jnp.zeros_like(lane)
        for u in range(16):
            p, y = member_place(u // 8, u // 2 % 4)
            block = layout[ctx_of(me.core, p, me.r, y) * 2 + u % 2]
            q_pos += jnp.where(row == u, block * half, 0)
            wanted = jnp.where(lane == u, block, wanted)

        def place(b, state):
            where_is, held = state
            block = layout[b]
            return jnp.where(lane == block, b, where_is), jnp.where(lane == b, block, held)

        def walk(j, state):
            at, first, low = state
            first = jnp.where(lane * half >= at, at, first)
            low = jnp.where(q_pos >= at, at, low)
            return at + lengths[j], first, low

        none = jnp.zeros_like(lane)
        where_is, held = lax.fori_loop(0, layout.shape[0], place, (none, none))
        _, first, low = lax.fori_loop(
            0, lengths.shape[0], walk, (jnp.int32(0), none, jnp.zeros_like(q_pos))
        )
        table[0:1, :] = where_is
        table[1:2, :] = first // half
        table[2:3, :] = held
        device = where_is // 2
        z, x, y = device // 8, device // 2 % 4, device % 2
        p, r = z * (1 - me.core) + x * me.core, x * (1 - me.core) + z * me.core
        table[3:4, :] = r * 8 + (y * 2 + (p + 1) // 2 % 2) * 2 + where_is % 2
        table[5:6, :] = wanted
        table[4:5, :] = jnp.where(p // 2 == me.pair, 1, 0)
        lows[...] = low

    def spread(i, a):
        to = me.member(i)
        dst = qh.at[me.pair, me.m] if a == 2 else kv.at[me.r, me.m, a]
        return remote(
            (k, v, q)[a].at[:, head_columns(to)], dst,
            s_send.at[i - 1, a], s_recv.at[i - 1, a], me.at_member(to),
        )

    def ring(i, j, rel, origin, to):
        slot = kv.at[origin, me.member(i), j]
        return remote(slot, slot, g_send.at[i, j, rel], g_recv.at[i, j, rel], me.at_ring(to))

    def twin(i):
        slot = qh.at[me.pair, me.member(i)]
        return remote(slot, slot, t_send.at[i], t_recv.at[i], me.at_twin())

    def arrived(i, j, rel):
        ring(i, j, rel, me.r, right).wait_recv()

    def weights_across(n):
        to = (me.across, me.diagonal)[n]
        place = (me.r, me.p)[n]
        rows = pl.ds(pl.multiple_of(place * quarter, quarter), quarter)
        return remote(
            w.at[rows, weight_columns(to)], w_far.at[me.core],
            w_send.at[n], w_recv.at[n], me.at_tp(to),
        )

    weights_to_mate = remote(
        w.at[:, weight_columns(me.mate)], w_near.at[1], w_send.at[2], w_recv.at[2], me.at_tp(me.mate)
    )
    for a in (2, 0, 1):
        for i in (2, 3, 1):
            start(spread(i, a))

    def pass_query(i):
        if i == 0:
            own[2].wait()
        else:
            spread(i, 2).wait_recv()
        start(twin(i))

    def pass_weights():
        start(weights_across(0))
        start(weights_across(1))
        start(weights_to_mate)

    for i in range(5):
        if i < 4:
            for j in (0, 1):
                if i == 0:
                    own[j].wait()
                else:
                    spread(i, j).wait_recv()
                start(ring(i, j, 0, me.r, right))
                start(ring(i, j, 1, me.r, left))
        if i == 0:
            pass_query(0)
            make_tables()
            pass_query(1)
        if i == 1:
            pass_query(2)
            pass_query(3)
        if i == 2:
            pass_weights()
        if i >= 1:
            arrived(i - 1, 0, 0)
            start(ring(i - 1, 0, 2, left, right))
            arrived(i - 1, 1, 1)
            start(ring(i - 1, 1, 2, right, left))
    own[3].wait()
    for i in range(4):
        arrived(i, 0, 1)
        arrived(i, 1, 0)
        arrived(i, 0, 2)
        arrived(i, 1, 2)
        twin(i).wait_recv()
    weights_across(0).wait_recv()
    weights_across(1).wait_recv()
    weights_to_mate.wait_recv()
    for copy in sends:
        copy.wait_send()


def gather(q, k, v, w, lengths, layout):
    rows, depth, columns = q.shape[0], w.shape[0], w.shape[1] // 4
    anywhere, near = pl.BlockSpec(memory_space=pltpu.HBM), pl.BlockSpec(memory_space=pltpu.VMEM)
    dma = pltpu.SemaphoreType.DMA
    return pl.pallas_call(
        gather_kernel,
        name="spread_and_gather",
        out_shape=(
            jax.ShapeDtypeStruct((2, 4, rows, HEAD), q.dtype),
            jax.ShapeDtypeStruct((4, 4, 2, rows, HEAD), q.dtype),
            jax.ShapeDtypeStruct((2, depth, columns), w.dtype),
            jax.ShapeDtypeStruct((2, depth // 4, columns), w.dtype),
            jax.ShapeDtypeStruct((8, 128), jnp.int32),
            jax.ShapeDtypeStruct((16, rows // 2), jnp.int32),
        ),
        in_specs=[anywhere] * 6,
        out_specs=(near,) * 6,
        scratch_shapes=[
            pltpu.SMEM(lengths.shape, jnp.int32),
            pltpu.SMEM(layout.shape, jnp.int32),
            dma((2,)),
            dma((4,)), dma((3, 3)), dma((3, 3)), dma((4, 2, 3)), dma((4, 2, 3)), dma((4,)), dma((4,)),
            dma((3,)), dma((3,)),
        ],
        compiler_params=pltpu.CompilerParams(
            collective_id=0, has_side_effects=True, vmem_limit_bytes=VMEM_BYTES
        ),
    )(q, k, v, w, lengths, layout)


def attend_kernel(
    near_table, lows, q, kv, out, logs, table, work, count, top, total, summed, table_sem
):
    blocks = BLOCKS
    half = q.shape[2] // 2
    spare = 16
    fetch = pltpu.make_async_copy(near_table, table, table_sem.at[0])
    fetch.start()
    top[...] = jnp.full(top.shape, LEAST, jnp.float32)
    total[...] = jnp.zeros(total.shape, jnp.float32)
    summed[...] = jnp.zeros(summed.shape, jnp.float32)
    for n in range(STREAMS):
        count[n] = 0
    fetch.wait()

    def query_block(u):
        return table[5, u]

    def plan(u, _):
        block = query_block(u)
        stream = jnp.int32(0)
        for n in range(1, STREAMS):
            stream = jnp.where(count[n] < count[stream], n, stream)

        def add(key_block, filled):
            work[stream, filled] = (u * blocks + key_block) * 32 + table[3, key_block]
            return filled + table[4, key_block]

        count[stream] = lax.fori_loop(
            table[1, block], block + 1, add, count[stream]
        )
        return 0

    lax.fori_loop(0, 16, plan, 0)
    steps = count[0]
    for n in range(1, STREAMS):
        steps = jnp.maximum(steps, count[n])
    for n in range(STREAMS):

        def fill(t, _):
            work[n, t] = (spare + n) * blocks * 32
            return 0

        lax.fori_loop(count[n], steps, fill, 0)

    def step(t, _):
        todo = []
        for n in range(STREAMS):
            code = work[n, t]
            slot = code & 31
            key_block = (code >> 5) & (blocks - 1)
            u = code >> 11
            real = jnp.minimum(u, spare - 1)
            q_rows = pl.ds(pl.multiple_of((real & 1) * half, half), half)
            k_rows = pl.ds(pl.multiple_of((slot & 1) * half, half), half)
            r_k, m_k = slot >> 3, (slot >> 1) & 3
            query = q[real >> 3, (real >> 1) & 3, q_rows, :]
            key, value = kv[r_k, m_k, 0, k_rows, :], kv[r_k, m_k, 1, k_rows, :]
            q_pos = query_block(real) * half + lax.broadcasted_iota(jnp.int32, (1, half), 1)
            todo.append((u, key_block, query, key, value, q_pos, lows[pl.ds(real, 1), :]))
        scores = [
            lax.dot_general(key, query, (((1,), (1,)), ((), ())), preferred_element_type=jnp.float32)
            for _, _, query, key, _, _, _ in todo
        ]
        for n, (u, key_block, _, _, value, q_pos, low) in enumerate(todo):
            k_pos = key_block * half + lax.broadcasted_iota(jnp.int32, (half, half), 0)
            masked = jnp.where((k_pos >= low) & (k_pos <= q_pos), scores[n], -1e30)
            old = top[u]
            new = jnp.maximum(old, jnp.max(masked, axis=0, keepdims=True))
            weights = jnp.exp2((masked - new) * (SCALE * LOG2E))
            factor = jnp.exp2((old - new) * (SCALE * LOG2E))
            top[u] = new
            total[u] = total[u] * factor + jnp.sum(weights, axis=0, keepdims=True)
            summed[u] = summed[u] * factor + lax.dot_general(
                value,
                weights.astype(jnp.bfloat16),
                (((0,), (0,)), ((), ())),
                preferred_element_type=jnp.float32,
            )
        return 0

    lax.fori_loop(0, steps, step, 0)

    def finish(u, _):
        at = (lax.div(u, 8), lax.rem(lax.div(u, 2), 4))
        rows = pl.ds(pl.multiple_of(lax.rem(u, 2) * half, half), half)
        some = total[u] > 0.0
        safe = jnp.where(some, total[u], 1.0)
        attended = (summed[u] * (1.0 / safe)).astype(out.dtype)
        for e in range(half // PART):
            chunk = lax.rem(u, 2) * (half // PART) + e
            out[at[0], at[1], chunk] = attended[:, e * PART : (e + 1) * PART]
        logs[at[0], at[1], :, rows] = jnp.where(some, top[u] * SCALE + jnp.log(safe), -1e30)
        return 0

    lax.fori_loop(0, 16, finish, 0)


def attend(table, lows, q, kv):
    rows = q.shape[2]
    half = rows // 2
    near = pl.BlockSpec(memory_space=pltpu.VMEM)
    return pl.pallas_call(
        attend_kernel,
        name="attend",
        out_shape=(
            jax.ShapeDtypeStruct((2, 4, rows // PART, HEAD, PART), q.dtype),
            jax.ShapeDtypeStruct((2, 4, 1, rows), jnp.float32),
        ),
        in_specs=[near] * 4,
        out_specs=(near, near),
        scratch_shapes=[
            pltpu.SMEM(table.shape, jnp.int32),
            pltpu.SMEM((STREAMS, 16 * BLOCKS + 1), jnp.int32),
            pltpu.SMEM((STREAMS,), jnp.int32),
            pltpu.VMEM((16 + STREAMS, 1, half), jnp.float32),
            pltpu.VMEM((16 + STREAMS, 1, half), jnp.float32),
            pltpu.VMEM((16 + STREAMS, HEAD, half), jnp.float32),
            pltpu.SemaphoreType.DMA((1,)),
        ],
        compiler_params=pltpu.CompilerParams(vmem_limit_bytes=VMEM_BYTES),
    )(table, lows, q, kv)


def project_kernel(
    o, logs, w_near, w_quarter, mixed, log_out,
    o_in, lo_in, merged, merged_logs, att, att_in, logs_in, w_far, total,
    own_sem, b_send, b_recv, lb_sem, a_send, a_recv, l_send, l_recv, x_send, x_recv, w_send, w_recv,
):
    me = Place()
    chunks = o.shape[2]
    left, right = lax.rem(me.r + 3, 4), lax.rem(me.r + 1, 4)
    wait_all = greet(
        [me.at_member(me.member(i)) for i in (1, 2, 3)]
        + [me.at_ring(left), me.at_ring(right), me.at_twin()]
        + [me.at_tp(me.mate), me.at_tp(me.across)]
    )
    own = [
        pltpu.make_async_copy(w_quarter.at[n], w_far.at[n, me.r], own_sem.at[n]) for n in (0, 1)
    ]
    for copy in own:
        copy.start()
    wait_all()
    sends = []

    def start(copy):
        copy.start()
        sends.append(copy)

    order = (3, 1, 2, 0)

    def to_twin(i, c):
        m = me.member(i)
        return remote(
            o.at[1 - me.pair, m, c], o_in.at[m, c], b_send.at[i, c], b_recv.at[i, c], me.at_twin()
        )

    def to_owner(i, c):
        return remote(
            merged.at[i - 1, c], att.at[c, :, head_columns(me.m)],
            a_send.at[i - 1, c], a_recv.at[i - 1, c], me.at_member(me.member(i)),
        )

    def log_to_owner(i):
        return remote(
            merged_logs.at[i], logs_in.at[me.m],
            l_send.at[i - 1], l_recv.at[i - 1], me.at_member(me.member(i)),
        )

    def pass_att(n, c):
        src = att_in.at[0, c] if n == 2 else att.at[c]
        to = me.across if n == 0 else me.mate
        return remote(src, att_in.at[n, c], x_send.at[n, c], x_recv.at[n, c], me.at_tp(to))

    def weights(n, rel, origin, to):
        slot = w_far.at[n, origin]
        return remote(slot, slot, w_send.at[n, rel], w_recv.at[n, rel], me.at_ring(to))

    def weights_arrived(n, rel):
        weights(n, rel, me.r, right).wait_recv()

    twin_logs = remote(logs.at[1 - me.pair], lo_in, lb_sem.at[0], lb_sem.at[1], me.at_twin())
    start(twin_logs)
    for c in range(chunks):
        for i in order:
            start(to_twin(i, c))
    twin_logs.wait_recv()
    shares = []
    for i in range(4):
        m = me.member(i)
        one, two = logs[me.pair, m], lo_in[m]
        most = jnp.maximum(one, two)
        e_one, e_two = jnp.exp(one - most), jnp.exp(two - most)
        both = e_one + e_two
        final = most + jnp.log(both)
        share = 1.0 / both
        shares.append((e_one * share, e_two * share))
        if i == 0:
            logs_in[me.m] = final
        else:
            merged_logs[i] = final
            start(log_to_owner(i))

    def merge(c):
        for i in order:
            m = me.member(i)
            lanes = slice(c * PART, (c + 1) * PART)
            to_twin(i, c).wait_recv()
            whole = (
                o[me.pair, m, c].astype(jnp.float32) * shares[i][0][:, lanes]
                + o_in[m, c].astype(jnp.float32) * shares[i][1][:, lanes]
            )
            turned = whole.T.astype(jnp.bfloat16)
            if i == 0:
                att[c, :, head_columns(me.m)] = turned
            else:
                merged[i - 1, c] = turned
                start(to_owner(i, c))

    def share_out(c):
        for i in (1, 2, 3):
            to_owner(i, c).wait_recv()
        start(pass_att(0, c))
        start(pass_att(1, c))
        total[c] = jnp.dot(att[c], w_near[0], preferred_element_type=jnp.float32)

    def far_weights(n):
        return w_far[n].reshape(w_near.shape[1:])

    def cross(c):
        pass_att(1, c).wait_recv()
        total[c] += jnp.dot(att_in[1, c], w_near[1], preferred_element_type=jnp.float32)
        pass_att(0, c).wait_recv()
        start(pass_att(2, c))

    def finish(c):
        both = total[c] + jnp.dot(
            att_in[0, c], far_weights(me.core), preferred_element_type=jnp.float32
        )
        pass_att(2, c).wait_recv()
        both += jnp.dot(
            att_in[2, c], far_weights(1 - me.core), preferred_element_type=jnp.float32
        )
        mixed[c * PART : (c + 1) * PART, :] = both.astype(mixed.dtype)

    for t in range(chunks + 3):
        if t < chunks:
            merge(t)
        if t == 0:
            for n in (0, 1):
                own[n].wait()
                start(weights(n, 0, me.r, right))
                start(weights(n, 1, me.r, left))
        if 0 <= t - 1 < chunks:
            share_out(t - 1)
        if t == 3:
            weights_arrived(0, 0)
            start(weights(0, 2, left, right))
            weights_arrived(1, 1)
            start(weights(1, 2, right, left))
        if 0 <= t - 2 < chunks:
            cross(t - 2)
        if t == chunks + 1:
            weights_arrived(0, 1)
            weights_arrived(1, 0)
            weights_arrived(0, 2)
            weights_arrived(1, 2)
            for c in range(chunks - 1):
                finish(c)
    finish(chunks - 1)
    for i in (1, 2, 3):
        log_to_owner(i).wait_recv()
    for h in range(4):
        log_out[h : h + 1, :] = logs_in[h]
    for copy in sends:
        copy.wait_send()


def project(o, logs, w_near, w_quarter):
    chunks, depth, columns = o.shape[2], w_near.shape[1], w_near.shape[2]
    rows = chunks * PART
    near = pl.BlockSpec(memory_space=pltpu.VMEM)
    dma = pltpu.SemaphoreType.DMA
    return pl.pallas_call(
        project_kernel,
        name="return_and_project",
        out_shape=(
            jax.ShapeDtypeStruct((rows, columns), jnp.bfloat16),
            jax.ShapeDtypeStruct((4, rows), jnp.float32),
        ),
        in_specs=[near] * 4,
        out_specs=(near, near),
        scratch_shapes=[
            pltpu.VMEM((4, chunks, HEAD, PART), jnp.bfloat16),
            pltpu.VMEM((4, 1, rows), jnp.float32),
            pltpu.VMEM((3, chunks, PART, HEAD), jnp.bfloat16),
            pltpu.VMEM((4, 1, rows), jnp.float32),
            pltpu.VMEM((chunks, PART, depth), jnp.bfloat16),
            pltpu.VMEM((3, chunks, PART, depth), jnp.bfloat16),
            pltpu.VMEM((4, 1, rows), jnp.float32),
            pltpu.VMEM((2, 4, depth // 4, columns), jnp.bfloat16),
            pltpu.VMEM((chunks, PART, columns), jnp.float32),
            dma((2,)), dma((4, chunks)), dma((4, chunks)), dma((2,)), dma((3, chunks)),
            dma((3, chunks)), dma((3,)), dma((3,)), dma((3, chunks)), dma((3, chunks)),
            dma((2, 3)), dma((2, 3)),
        ],
        compiler_params=pltpu.CompilerParams(
            collective_id=1, has_side_effects=True, vmem_limit_bytes=VMEM_BYTES
        ),
    )(o, logs, w_near, w_quarter)


def local(queries, keys, values, out_weight, doc_lengths, layout):
    held = (
        pltpu.with_memory_space_constraint(t, pltpu.HBM)
        for t in (queries, keys, values, out_weight, doc_lengths, layout)
    )
    qh, kv, w_near, w_quarter, table, lows = gather(*held)
    o, logs = attend(table, lows, qh, kv)
    return project(o, logs, w_near, w_quarter)


def solution(mesh):
    placed = (P("ctx", "tp"), P("ctx", "tp"), P("ctx", "tp"), P("tp", None), P(), P())
    return jax.shard_map(
        local,
        mesh=mesh,
        in_specs=placed,
        out_specs=(P("ctx", "tp"), P("tp", "ctx")),
        check_vma=False,
    )
```
